256 devices in a mesh: sec: 8 (over y, core), blk: 32 (over z, x).
Axes of the slice: x: 4, y: 4, z: 8, core: 2. Of those that a mesh axis runs over, the one named last changes fastest.
Arguments:
- env_left: bfloat16 [26, 32, 128, 128], P(None, 'blk'), may hold values from -6 to 6
- transfer: bfloat16 [8, 32, 3, 128, 128], P('sec', 'blk'), may hold values from -0.375 to 0.375
- mpo_mix: float32 [8, 26, 26], P('sec'), may hold values from -1.25 to 1.25
- right_env: bfloat16 [8, 26, 32, 128, 128], P('sec', None, 'blk'), may hold values from -1 to 1
- start_state: float32 [8, 32, 128, 128], P('sec', 'blk'), may hold values from -0.00015258789 to 0.00015258789
- block_rank: int32 [32], P('blk'), may hold values from 1 to 128, as said below
Outputs:
- state: float32 [8, 32, 128, 128], P('sec', 'blk')
- environment: bfloat16 [8, 26, 32, 128, 128], P('sec', None, 'blk')
The draws below stay inside these ranges and needn't reach their ends.
Inputs may be any that keep to these rules, and one draw needn't show every extreme that they name: `block_rank`: one block has rank exactly 128.
All inputs are finite; a program needn't handle non-finite values.
Results may differ from the reference program's by a relative error of at most 0.04.
Values may be sent and summed in bfloat16 or wider, within the bound.
A program may use at most 64 MiB of HBM per device.

```python
import jax
import jax.numpy as jnp
from jax import lax

B = 128
WM = 26
ITERS = 4
NQ = 32
N_SEC = 8


def rank_table(key):
    ranks_key = jax.random.fold_in(key, 7)
    ranks = jax.random.randint(ranks_key, (NQ,), B // 4, B + 1)
    return ranks.at[0].set(B).astype(jnp.int32)


def draw_block_rank(key, part):
    return rank_table(key)


def draw_right_env(key, part):
    ranks = rank_table(key)
    key = jax.random.fold_in(key, 13)
    shape = (N_SEC, WM, NQ, B, B)
    scale = (16.0 * WM * B) ** (-0.5)
    values = jax.random.truncated_normal(key, -6.0, 6.0, shape, jnp.float32)
    factor = jnp.float32(B) / ranks.astype(jnp.float32)
    result = values * scale * factor[None, None, :, None, None]
    return result.astype(jnp.bfloat16)


def block_levels(key, dims, shards, smallest, largest):
    factor_of, own = 1.0, jax.random.fold_in(key, 6)
    for position, blocks in shards:
        steps = jnp.exp(jax.random.uniform(jax.random.fold_in(own, position), (blocks,), jnp.float32, smallest / len(shards), largest / len(shards)))
        factor_of = factor_of * jnp.repeat(steps, dims[position] // blocks).reshape([-1 if axis == position else 1 for axis in range(len(dims))])
    return factor_of


def normal_values(own_key, extent, deviation, most, shards=(), kind=jnp.bfloat16):
    array = deviation * jax.random.normal(own_key, extent, jnp.float32)
    if shards:
        array = array * block_levels(own_key, extent, shards, -0.22, 0.18)
    return jnp.clip(array, -most, most).astype(kind)


def setup_inputs(seed: int = 0) -> dict:
    keys = jax.random.split(jax.random.key(seed), 7)
    return {
        "env_left": normal_values(keys[0], (WM, NQ, B, B), 1.0, 6.0, ((1, 32),)),
        "transfer": normal_values(keys[1], (N_SEC, NQ, 3, B, B), (7 * B // 4) ** -0.5, 0.375, ((0, 8), (1, 32))),
        "mpo_mix": normal_values(keys[2], (N_SEC, WM, WM), WM ** -0.5, 1.25, ((0, 8),), jnp.float32),
        "right_env": draw_right_env(jax.random.fold_in(keys[6], 71), 0),
        "start_state": normal_values(keys[4], (N_SEC, NQ, B, B), 0.00001, 0.00015258789, ((0, 8), (1, 32)), jnp.float32),
        "block_rank": draw_block_rank(jax.random.fold_in(keys[6], 71), 0),
    }


def step_env(env, trans, mix):
    zero = jnp.zeros((WM, 1, B, B), jnp.bfloat16)
    padded = jnp.concatenate([zero, env, zero], axis=1)
    total = jnp.zeros((WM, NQ, B, B), jnp.float32)
    for d in range(3):
        source = padded[:, d:d + NQ].astype(jnp.float32)
        tensor = trans[:, d].astype(jnp.float32)
        left = jnp.einsum('qji,wqjk->wqik', tensor, source).astype(jnp.bfloat16)
        total = total + jnp.einsum('wqik,qkl->wqil', left.astype(jnp.float32), tensor)
    mixed = jnp.einsum('vw,wqil->vqil', mix, total, precision=lax.Precision.HIGHEST)
    return mixed.astype(jnp.bfloat16)

def reference(env_left, transfer, mpo_mix, right_env, start_state, block_rank):
    envs = [env_left]
    for s in range(N_SEC - 1):
        envs.append(step_env(envs[-1], transfer[s], mpo_mix[s]))
    environment = jnp.stack(envs)
    index = jnp.arange(B, dtype=jnp.int32)
    keep = (index[None, :] < block_rank[:, None]).astype(jnp.float32)
    mask = keep[:, :, None] * keep[:, None, :]
    states = []
    for s in range(N_SEC):
        psi = start_state[s] * mask
        env = environment[s].astype(jnp.float32)
        renv = right_env[s].astype(jnp.float32)
        for step in range(ITERS):
            value = psi.astype(jnp.bfloat16).astype(jnp.float32)
            left = jnp.einsum('wqij,qjk->wqik', env, value).astype(jnp.bfloat16)
            applied = jnp.einsum('wqik,wqkl->qil', left.astype(jnp.float32), renv)
            zero = jnp.zeros((1, B, B), jnp.float32)
            padded = jnp.concatenate([zero, psi, zero], axis=0)
            applied = applied + 0.5 * (padded[:-2] + padded[2:])
            psi = applied * mask
            total = jnp.sum(psi * psi) / (NQ * B * B)
            psi = psi / jnp.sqrt(total + 1e-06)
        states.append(psi)
    return (jnp.stack(states), environment)
```

```python
import jax
import jax.numpy as jnp
from jax import lax
from jax.experimental import pallas as pl
from jax.experimental.pallas import tpu as pltpu
from jax.sharding import PartitionSpec as P

ITERS = 4
B = 128
WM = 26
NS = 8
NQ = 32
SLOTS = 4
STEPS = NS - 1
PAIRS = WM // 2
ROWS = 16
KR = WM * ROWS
MESH = pl.DeviceIdType.MESH
F32 = jnp.float32
BF16 = jnp.bfloat16


def dot(a, b):
    return jnp.dot(a, b, preferred_element_type=F32)


def kernel(
    env_hbm, trans, mix, renv_hbm, start, rank, state, env_out,
    raw, halo_l, halo_r, recv, envm, renv, tall, tt, mixall, amat, own_mix,
    xsend, xl, xr, psend, pall,
    load_sem, renv_sem, out_sem, recv_sem, deliver_sem, local_sem,
    hrecv, hsend, trecv, tsend, fsend, mrecv, msend,
    xrecv, xsem, precv, psem,
):
    g = lax.axis_index("sec")
    q = lax.axis_index("blk")
    y = g // 2
    core = lax.rem(g, 2)
    right = lax.rem(q + 1, NQ)
    left = lax.rem(q + NQ - 1, NQ)
    first = 3 * g + jnp.where(g >= 1, 1, 0) + jnp.where(g >= 3, 1, 0)
    four = jnp.logical_or(g == 0, g == 2)

    barrier = pltpu.get_barrier_semaphore()

    def greet_sec(i, carry):
        pl.semaphore_signal(barrier, inc=1, device_id=(lax.rem(g + i, NS), q), device_id_type=MESH)
        return carry

    def greet_blk(i, carry):
        pl.semaphore_signal(barrier, inc=1, device_id=(g, lax.rem(q + i, NQ)), device_id_type=MESH)
        return carry

    lax.fori_loop(1, NS, greet_sec, 0)
    lax.fori_loop(1, NQ, greet_blk, 0)

    def each_slot(j, body):
        if j < SLOTS - 1:
            body()
        else:
            pl.when(four)(body)

    def load(j):
        return pltpu.make_async_copy(env_hbm.at[first + j], raw.at[0, j], load_sem.at[j])

    for j in range(SLOTS):
        each_slot(j, lambda j=j: load(j).start())

    @pl.when(g == 0)
    def _():
        def body(w, carry):
            pltpu.make_async_copy(env_hbm.at[w], recv.at[w], recv_sem.at[w]).start()
            return carry

        lax.fori_loop(0, WM, body, 0)

    renv_copy = pltpu.make_async_copy(renv_hbm, renv, renv_sem)
    renv_copy.start()

    own_mix[...] = jnp.zeros_like(own_mix)
    own_mix[:WM, :WM] = mix[...]
    tall[g] = trans[...]
    mixall[g] = own_mix[...]
    row = lax.broadcasted_iota(jnp.int32, (32, B), 0)
    col = lax.broadcasted_iota(jnp.int32, (32, B), 1)
    amat[...] = jnp.where(row == col, 1.0, 0.0).astype(F32)
    for j in range(SLOTS):
        each_slot(j, lambda j=j: load(j).wait())

    pl.semaphore_wait(barrier, NS - 1 + NQ - 1)

    def halo_copies(s, j):
        to_right = pltpu.make_async_remote_copy(
            src_ref=raw.at[s, j], dst_ref=halo_l.at[s, j],
            send_sem=hsend.at[s, 0, j], recv_sem=hrecv.at[s, 0, j],
            device_id=(g, right), device_id_type=MESH,
        )
        to_left = pltpu.make_async_remote_copy(
            src_ref=raw.at[s, j], dst_ref=halo_r.at[s, j],
            send_sem=hsend.at[s, 1, j], recv_sem=hrecv.at[s, 1, j],
            device_id=(g, left), device_id_type=MESH,
        )
        return to_right, to_left

    def trans_copy(src, s, sem, other):
        return pltpu.make_async_remote_copy(
            src_ref=src, dst_ref=tall.at[s], send_sem=sem, recv_sem=trecv.at[s],
            device_id=(other, q), device_id_type=MESH,
        )

    def mix_copy(i):
        return pltpu.make_async_remote_copy(
            src_ref=own_mix, dst_ref=mixall.at[g], send_sem=msend.at[i], recv_sem=mrecv.at[g],
            device_id=(lax.rem(g + i, NS), q), device_id_type=MESH,
        )

    def sends_trans(i):
        near = jnp.logical_or(lax.rem(i, 2) == 0, g + i == g + 1 - 2 * core)
        return near

    def each_trans(act):
        @pl.when(g == 0)
        def _():
            for i in range(1, NS):
                act(trans_copy(trans, 0, tsend.at[i], i))

        @pl.when(jnp.logical_and(g > 0, g < STEPS))
        def _():
            act(trans_copy(trans, g, tsend.at[0], g + 1 - 2 * core))
            for i in range(1, 4):
                act(trans_copy(trans, g, tsend.at[i], lax.rem(g + 2 * i, NS)))

    each_trans(lambda c: c.start())
    for j in range(SLOTS):
        def body(j=j):
            for c in halo_copies(0, j):
                c.start()
        each_slot(j, body)

    @pl.when(g < STEPS)
    def _():
        for i in range(1, NS):
            mix_copy(i).start()

    def deliver(s, j):
        return pltpu.make_async_remote_copy(
            src_ref=raw.at[s, j], dst_ref=recv.at[first + j],
            send_sem=deliver_sem.at[s, j], recv_sem=recv_sem.at[first + j],
            device_id=(s, q), device_id_type=MESH,
        )

    def deliver_local(s, j):
        return pltpu.make_async_copy(raw.at[s, j], recv.at[first + j], recv_sem.at[first + j])

    def forwards(s):
        return jnp.logical_and(
            jnp.logical_and(core == lax.rem(s, 2), y != s // 2), jnp.logical_and(s >= 1, s < STEPS)
        )

    def forward(s):
        return trans_copy(tall.at[s], s, fsend.at[s], g + 1 - 2 * core)

    def wait_trans(s):
        pltpu.make_async_copy(tall.at[s], tall.at[s], trecv.at[s]).wait()

    def step(s, carry):
        @pl.when(jnp.logical_and(g != s, jnp.logical_not(forwards(s))))
        def _():
            wait_trans(s)

        @pl.when(forwards(s + 1))
        def _():
            wait_trans(s + 1)
            forward(s + 1).start()

        for d in range(3):
            t = tall[s, d * B:(d + 1) * B, :].T
            if d == 0:
                t = jnp.where(q > 0, t, jnp.zeros_like(t))
            if d == 2:
                t = jnp.where(q < NQ - 1, t, jnp.zeros_like(t))
            tt[d] = t

        for j in range(SLOTS):
            def body(j=j):
                for c in halo_copies(s, j):
                    c.wait_recv()
                parts = [halo_l[s, j], raw[s, j], halo_r[s, j]]
                parts = [dot(tt[d], parts[d]).astype(BF16) for d in range(3)]
                out = dot(jnp.concatenate(parts, axis=1), tall[s])
                raw[s + 1, j] = out.astype(BF16)

                @pl.when(s < STEPS - 1)
                def _():
                    for c in halo_copies(s + 1, j):
                        c.start()

                @pl.when(g != s + 1)
                def _():
                    deliver(s + 1, j).start()

                @pl.when(g == s + 1)
                def _():
                    deliver_local(s + 1, j).start()

            each_slot(j, body)

        @pl.when(g != s)
        def _():
            pltpu.make_async_copy(mixall.at[s], mixall.at[s], mrecv.at[s]).wait()

        @pl.when(s < g)
        def _():
            amat[...] = jnp.dot(mixall[s][:, :32], amat[...], precision=lax.Precision.HIGHEST, preferred_element_type=F32)

        return carry

    lax.fori_loop(0, STEPS, step, 0)

    a = amat[...][:, :32].astype(BF16)
    wide = lax.broadcasted_iota(jnp.int32, (KR, 32), 0) // ROWS
    spread = jnp.where(wide == lax.broadcasted_iota(jnp.int32, (KR, 32), 1), 1.0, 0.0).astype(BF16)
    big = dot(spread, a).astype(BF16)
    big = lax.dot_general(big, spread, (((1,), (1,)), ((), ())), preferred_element_type=F32)
    r0 = lax.rem(lax.broadcasted_iota(jnp.int32, (KR, KR), 0), ROWS)
    r1 = lax.rem(lax.broadcasted_iota(jnp.int32, (KR, KR), 1), ROWS)
    big = jnp.where(r0 == r1, big, 0.0).astype(BF16)

    def wait_recv(w, carry):
        pltpu.make_async_copy(recv.at[w], recv.at[w], recv_sem.at[w]).wait()
        return carry

    lax.fori_loop(0, WM, wait_recv, 0)
    for t in range(B // ROWS):
        rows = recv[:, t * ROWS:(t + 1) * ROWS, :].reshape(KR, B)
        envm[:, t * ROWS:(t + 1) * ROWS, :] = dot(big, rows).astype(BF16).reshape(WM, ROWS, B)
    out_copy = pltpu.make_async_copy(envm, env_out, out_sem)
    out_copy.start()
    renv_copy.wait()

    keep0 = lax.broadcasted_iota(jnp.int32, (B, B), 0) < rank[0]
    keep1 = lax.broadcasted_iota(jnp.int32, (B, B), 1) < rank[0]
    mask = jnp.where(jnp.logical_and(keep0, keep1), 1.0, 0.0).astype(F32)

    def x_copies(k):
        to_right = pltpu.make_async_remote_copy(
            src_ref=xsend.at[k], dst_ref=xl.at[k], send_sem=xsem.at[k, 0], recv_sem=xrecv.at[k, 0],
            device_id=(g, right), device_id_type=MESH,
        )
        to_left = pltpu.make_async_remote_copy(
            src_ref=xsend.at[k], dst_ref=xr.at[k], send_sem=xsem.at[k, 1], recv_sem=xrecv.at[k, 1],
            device_id=(g, left), device_id_type=MESH,
        )
        return to_right, to_left

    def sum_copy(k, i):
        return pltpu.make_async_remote_copy(
            src_ref=psend.at[k], dst_ref=pall.at[k, q], send_sem=psem.at[k], recv_sem=precv.at[k],
            device_id=(g, lax.rem(q + i, NQ)), device_id_type=MESH,
        )

    def start_sum(k, part):
        psend[k] = part
        pall[k, q] = part

        def body(i, carry):
            sum_copy(k, i).start()
            return carry

        lax.fori_loop(1, NQ, body, 0)

    def finish_sum(k):
        others = pall.at[k, pl.ds(0, NQ - 1)]
        pltpu.make_async_copy(others, others, precv.at[k]).wait()
        total = jnp.sum(jnp.sum(pall[k], axis=0), axis=1, keepdims=True)
        return lax.rsqrt(total / (NQ * B * B) + 1e-06)

    cur = start[...] * mask
    part = None
    for k in range(ITERS):
        xsend[k] = cur.astype(BF16)
        for c in x_copies(k):
            c.start()
        if k > 0:
            start_sum(k - 1, part)
            own = jnp.sum(part, axis=1, keepdims=True) / (B * B)
            sigma = lax.rsqrt(jnp.maximum(own, 1e-30))
            x = (cur * sigma).astype(BF16)
        else:
            x = cur.astype(BF16)
        zero = jnp.zeros_like(x)
        xx = jnp.concatenate([jnp.concatenate([x, zero], axis=1), jnp.concatenate([zero, x], axis=1)], axis=0)
        acc = None
        for p in range(PAIRS):
            pair = jnp.concatenate([envm[2 * p], envm[2 * p + 1]], axis=1)
            term = dot(dot(pair, xx).astype(BF16), renv[2 * p:2 * p + 2].reshape(2 * B, B))
            acc = term if acc is None else acc + term
        for c in x_copies(k):
            c.wait_recv()
        near_l = jnp.where(q > 0, xl[k].astype(F32), 0.0)
        near_r = jnp.where(q < NQ - 1, xr[k].astype(F32), 0.0)
        hop = 0.5 * (near_l + near_r)
        if k > 0:
            inv = finish_sum(k - 1)
            cur = mask * (acc * (inv / sigma) + hop * inv)
        else:
            cur = mask * (acc + hop)
        part = jnp.sum(cur * cur, axis=0, keepdims=True)
    start_sum(ITERS - 1, part)

    def drain(s, carry):
        for j in range(SLOTS):
            def body(j=j):
                for c in halo_copies(s, j):
                    c.wait_send()

                @pl.when(g != s + 1)
                def _():
                    deliver(s + 1, j).wait_send()

            each_slot(j, body)

        @pl.when(forwards(s))
        def _():
            forward(s).wait_send()

        return carry

    lax.fori_loop(0, STEPS, drain, 0)
    each_trans(lambda c: c.wait_send())

    @pl.when(g < STEPS)
    def _():
        for i in range(1, NS):
            mix_copy(i).wait_send()

    for k in range(ITERS):
        for c in x_copies(k):
            c.wait_send()
        others = pall.at[k, pl.ds(0, NQ - 1)]
        pltpu.make_async_copy(others, others, psem.at[k]).wait()
    out_copy.wait()
    state[...] = cur * finish_sum(ITERS - 1)


def per_device(env_left, transfer, mpo_mix, right_env, start_state, block_rank):
    dma = pltpu.SemaphoreType.DMA
    vmem = pl.BlockSpec(memory_space=pltpu.VMEM)
    anym = pl.BlockSpec(memory_space=pl.ANY)
    state, env = pl.pallas_call(
        kernel,
        out_shape=(
            jax.ShapeDtypeStruct((B, B), F32),
            jax.ShapeDtypeStruct((WM, B, B), BF16),
        ),
        in_specs=[anym, vmem, vmem, anym, vmem, pl.BlockSpec(memory_space=pltpu.SMEM)],
        out_specs=(vmem, anym),
        scratch_shapes=[
            pltpu.VMEM((NS, SLOTS, B, B), BF16),
            pltpu.VMEM((STEPS, SLOTS, B, B), BF16),
            pltpu.VMEM((STEPS, SLOTS, B, B), BF16),
            pltpu.VMEM((WM, B, B), BF16),
            pltpu.VMEM((WM, B, B), BF16),
            pltpu.VMEM((WM, B, B), BF16),
            pltpu.VMEM((NS, 3 * B, B), BF16),
            pltpu.VMEM((3, B, B), BF16),
            pltpu.VMEM((NS, 32, B), F32),
            pltpu.VMEM((32, B), F32),
            pltpu.VMEM((32, B), F32),
            pltpu.VMEM((ITERS, B, B), BF16),
            pltpu.VMEM((ITERS, B, B), BF16),
            pltpu.VMEM((ITERS, B, B), BF16),
            pltpu.VMEM((ITERS, 1, B), F32),
            pltpu.VMEM((ITERS, NQ, 1, B), F32),
            dma((SLOTS,)),
            dma,
            dma,
            dma((WM,)),
            dma((NS, SLOTS)),
            dma,
            dma((STEPS, 2, SLOTS)),
            dma((STEPS, 2, SLOTS)),
            dma((NS,)),
            dma((NS,)),
            dma((NS,)),
            dma((NS,)),
            dma((NS,)),
            dma((ITERS, 2)),
            dma((ITERS, 2)),
            dma((ITERS,)),
            dma((ITERS,)),
        ],
        compiler_params=pltpu.CompilerParams(
            collective_id=0, has_side_effects=True, vmem_limit_bytes=40 * 1024 * 1024
        ),
    )(
        env_left.reshape(WM, B, B),
        transfer.reshape(3 * B, B),
        mpo_mix.reshape(WM, WM),
        right_env.reshape(WM, B, B),
        start_state.reshape(B, B),
        block_rank,
    )
    return state.reshape(1, 1, B, B), env.reshape(1, WM, 1, B, B)


def solution(mesh):
    in_specs = (
        P(None, "blk", None, None),
        P("sec", "blk", None, None, None),
        P("sec", None, None),
        P("sec", None, "blk", None, None),
        P("sec", "blk", None, None),
        P("blk"),
    )
    out_specs = (P("sec", "blk", None, None), P("sec", None, "blk", None, None))
    return jax.shard_map(
        per_device, mesh=mesh, in_specs=in_specs, out_specs=out_specs, check_vma=False
    )
```

```python
import jax
import jax.numpy as jnp
from jax import lax
from jax.experimental import pallas as pl
from jax.experimental.pallas import tpu as pltpu
from jax.sharding import PartitionSpec as P

ITERS = 4
B = 128
WM = 26
NS = 8
NQ = 32
SLOTS = 4
STEPS = NS - 1
PAIRS = WM // 2
ROWS = 16
KR = WM * ROWS
FIRSTS = (0, 4, 7, 11, 14, 17, 20, 23)
ORDER = [f + j for j in range(3) for f in FIRSTS] + [3, 10]
GROUPS = (range(0, 4), range(4, 8), range(8, 13))
AUX = 16
MSG = B + AUX
SENDS = ((0, 1), (0, -1), (1, 1), (1, -1), (1, 2), (1, -2), (2, 1), (2, -1), (3, 1), (3, -1))
LOG_EPS = -19.931568569324174
LOG_N = 19.0
MESH = pl.DeviceIdType.MESH
F32 = jnp.float32
BF16 = jnp.bfloat16


def dot(a, b):
    return jnp.dot(a, b, preferred_element_type=F32)


def kernel(
    env_hbm, trans_hbm, mix_hbm, renv_hbm, start_hbm, rank, state, env_out,
    raw, halo_l, halo_r, recv, renv, renvp, tall, tt, mixall, amat, mix_in, own_mix,
    start, outbox, inbox, psend, pall,
    load_sem, in_sem, recv_sem, deliver_sem,
    hrecv, hsend, trecv, tsend, fsend, mrecv, msend,
    xrecv, xsem, precv, psem,
):
    g = lax.axis_index("sec")
    q = lax.axis_index("blk")
    y = g // 2
    core = lax.rem(g, 2)
    right = lax.rem(q + 1, NQ)
    left = lax.rem(q + NQ - 1, NQ)
    first = 3 * g + jnp.where(g >= 1, 1, 0) + jnp.where(g >= 3, 1, 0)
    four = jnp.logical_or(g == 0, g == 2)

    loads = [
        pltpu.make_async_copy(trans_hbm, tall.at[g], in_sem.at[0]),
        pltpu.make_async_copy(mix_hbm, mix_in, in_sem.at[1]),
        pltpu.make_async_copy(start_hbm, start, in_sem.at[2]),
        pltpu.make_async_copy(renv_hbm, renv, in_sem.at[3]),
    ]

    def each_slot(j, body):
        if j < SLOTS - 1:
            body()
        else:
            pl.when(four)(body)

    def load(j):
        return pltpu.make_async_copy(env_hbm.at[first + j], raw.at[0, j], load_sem.at[j])

    loads[0].start()
    for j in range(SLOTS):
        each_slot(j, lambda j=j: load(j).start())
    for c in loads[1:]:
        c.start()

    barrier = pltpu.get_barrier_semaphore()

    def greet_sec(i, carry):
        pl.semaphore_signal(barrier, inc=1, device_id=(lax.rem(g + i, NS), q), device_id_type=MESH)
        return carry

    def greet_blk(i, carry):
        pl.semaphore_signal(barrier, inc=1, device_id=(g, lax.rem(q + i, NQ)), device_id_type=MESH)
        return carry

    lax.fori_loop(1, NS, greet_sec, 0)
    lax.fori_loop(1, NQ, greet_blk, 0)

    @pl.when(g == 0)
    def _():
        def body(w, carry):
            pltpu.make_async_copy(env_hbm.at[w], recv.at[w], recv_sem.at[w]).start()
            return carry

        lax.fori_loop(0, WM, body, 0)

    own_mix[...] = jnp.zeros_like(own_mix)
    loads[1].wait()
    own_mix[:WM, :WM] = mix_in[...].reshape(WM, WM)
    mixall[g] = own_mix[...]
    row = lax.broadcasted_iota(jnp.int32, (32, B), 0)
    col = lax.broadcasted_iota(jnp.int32, (32, B), 1)
    amat[...] = jnp.where(row == col, 1.0, 0.0).astype(F32)
    keep0 = lax.broadcasted_iota(jnp.int32, (B, B), 0)
    keep1 = lax.broadcasted_iota(jnp.int32, (B, B), 1)
    larger = jnp.maximum(keep0, keep1).astype(F32)
    my_rank = rank[0].astype(F32)
    mask = jnp.where(larger < my_rank, 1.0, 0.0).astype(F32)
    loads[2].wait()
    outbox[0, :B, :] = (start[...] * mask).astype(BF16)
    outbox[0, B:, :] = jnp.full((AUX, B), my_rank, F32).astype(BF16)
    loads[0].wait()
    for j in range(SLOTS):
        each_slot(j, lambda j=j: load(j).wait())

    pl.semaphore_wait(barrier, NS - 1 + NQ - 1)

    def halo_copies(s, j):
        to_right = pltpu.make_async_remote_copy(
            src_ref=raw.at[s, j], dst_ref=halo_l.at[s, j],
            send_sem=hsend.at[s, 0, j], recv_sem=hrecv.at[s, 0, j],
            device_id=(g, right), device_id_type=MESH,
        )
        to_left = pltpu.make_async_remote_copy(
            src_ref=raw.at[s, j], dst_ref=halo_r.at[s, j],
            send_sem=hsend.at[s, 1, j], recv_sem=hrecv.at[s, 1, j],
            device_id=(g, left), device_id_type=MESH,
        )
        return to_right, to_left

    def trans_copy(src, s, sem, other):
        return pltpu.make_async_remote_copy(
            src_ref=src, dst_ref=tall.at[s], send_sem=sem, recv_sem=trecv.at[s],
            device_id=(other, q), device_id_type=MESH,
        )

    def mix_copy(i):
        return pltpu.make_async_remote_copy(
            src_ref=own_mix, dst_ref=mixall.at[g], send_sem=msend.at[i], recv_sem=mrecv.at[g],
            device_id=(lax.rem(g + i, NS), q), device_id_type=MESH,
        )

    def each_trans(act):
        @pl.when(g == 0)
        def _():
            for i in range(1, NS):
                act(trans_copy(tall.at[g], 0, tsend.at[i], i))

        @pl.when(jnp.logical_and(g > 0, g < STEPS))
        def _():
            act(trans_copy(tall.at[g], g, tsend.at[0], g + 1 - 2 * core))
            for i in range(1, 4):
                act(trans_copy(tall.at[g], g, tsend.at[i], lax.rem(g + 2 * i, NS)))

    each_trans(lambda c: c.start())
    for j in range(SLOTS):
        def body(j=j):
            for c in halo_copies(0, j):
                c.start()
        each_slot(j, body)

    @pl.when(g < STEPS)
    def _():
        for i in range(1, NS):
            mix_copy(i).start()

    def box_copy(i):
        m, far = SENDS[i]
        return pltpu.make_async_remote_copy(
            src_ref=outbox.at[m], dst_ref=inbox.at[i], send_sem=xsem.at[i], recv_sem=xrecv.at[i],
            device_id=(g, lax.rem(q + (NQ + far), NQ)), device_id_type=MESH,
        )

    def send(m):
        for i in range(len(SENDS)):
            if SENDS[i][0] == m:
                box_copy(i).start()

    send(0)

    def deliver(s, j):
        return pltpu.make_async_remote_copy(
            src_ref=raw.at[s, j], dst_ref=recv.at[first + j],
            send_sem=deliver_sem.at[s, j], recv_sem=recv_sem.at[first + j],
            device_id=(s, q), device_id_type=MESH,
        )

    def deliver_local(s, j):
        return pltpu.make_async_copy(raw.at[s, j], recv.at[first + j], recv_sem.at[first + j])

    def forwards(s):
        return jnp.logical_and(
            jnp.logical_and(core == lax.rem(s, 2), y != s // 2), jnp.logical_and(s >= 1, s < STEPS)
        )

    def forward(s):
        return trans_copy(tall.at[s], s, fsend.at[s], g + 1 - 2 * core)

    def wait_trans(s):
        pltpu.make_async_copy(tall.at[s], tall.at[s], trecv.at[s]).wait()

    def step(s, carry):
        @pl.when(jnp.logical_and(g != s, jnp.logical_not(forwards(s))))
        def _():
            wait_trans(s)

        @pl.when(forwards(s + 1))
        def _():
            wait_trans(s + 1)
            forward(s + 1).start()

        for d in range(3):
            t = tall[s, d * B:(d + 1) * B, :].T
            if d == 0:
                t = jnp.where(q > 0, t, jnp.zeros_like(t))
            if d == 2:
                t = jnp.where(q < NQ - 1, t, jnp.zeros_like(t))
            tt[d] = t

        for j in range(SLOTS):
            def body(j=j):
                for c in halo_copies(s, j):
                    c.wait_recv()
                parts = [halo_l[s, j], raw[s, j], halo_r[s, j]]
                parts = [dot(tt[d], parts[d]).astype(BF16) for d in range(3)]
                out = dot(jnp.concatenate(parts, axis=1), tall[s])
                raw[s + 1, j] = out.astype(BF16)

                @pl.when(s < STEPS - 1)
                def _():
                    for c in halo_copies(s + 1, j):
                        c.start()

                @pl.when(g != s + 1)
                def _():
                    deliver(s + 1, j).start()

                @pl.when(g == s + 1)
                def _():
                    deliver_local(s + 1, j).start()

            each_slot(j, body)

        @pl.when(g != s)
        def _():
            pltpu.make_async_copy(mixall.at[s], mixall.at[s], mrecv.at[s]).wait()

        @pl.when(s < g)
        def _():
            amat[...] = jnp.dot(mixall[s][:, :32], amat[...], precision=lax.Precision.HIGHEST, preferred_element_type=F32)

        return carry

    lax.fori_loop(0, STEPS, step, 0)

    a = amat[...][:, :32].astype(BF16)
    wide = lax.broadcasted_iota(jnp.int32, (KR, 32), 0) // ROWS
    spread = jnp.where(wide == lax.broadcasted_iota(jnp.int32, (KR, 32), 1), 1.0, 0.0).astype(BF16)
    r0 = lax.rem(lax.broadcasted_iota(jnp.int32, (KR, KR), 0), ROWS)
    r1 = lax.rem(lax.broadcasted_iota(jnp.int32, (KR, KR), 1), ROWS)

    def widen(half):
        full = lax.dot_general(half.astype(BF16), spread, (((1,), (1,)), ((), ())), preferred_element_type=F32)
        return jnp.where(r0 == r1, full, 0.0).astype(BF16)

    turned = widen(lax.dot_general(spread, a, (((1,), (1,)), ((), ())), preferred_element_type=F32))
    loads[3].wait()
    for t in range(B // ROWS):
        rows = renv[:, t * ROWS:(t + 1) * ROWS, :].reshape(KR, B)
        mixed = dot(turned, rows).astype(BF16).reshape(WM, ROWS, B)
        for i, w in enumerate(ORDER):
            at = (i % 2) * B + t * ROWS
            renvp[i // 2, at:at + ROWS, :] = mixed[w]
    big = widen(dot(spread, a))

    def pairs(xx, group):
        acc = None
        for p in group:
            pair = jnp.concatenate([recv[ORDER[2 * p]], recv[ORDER[2 * p + 1]]], axis=1)
            term = dot(dot(pair, xx).astype(BF16), renvp[p])
            acc = term if acc is None else acc + term
        return acc

    def twice(x):
        zero = jnp.zeros_like(x)
        return jnp.concatenate([jnp.concatenate([x, zero], axis=1), jnp.concatenate([zero, x], axis=1)], axis=0)

    def apply(x):
        return pairs(twice(x), range(PAIRS)) * mask

    def largest(v):
        return jnp.max(jnp.max(jnp.abs(v), axis=0, keepdims=True), axis=1, keepdims=True)

    def total(v):
        return jnp.sum(jnp.sum(v, axis=0, keepdims=True), axis=1, keepdims=True)

    def log2(v):
        return jnp.log(jnp.maximum(v, 1e-30)) * 1.4426950408889634

    def norm(v, e):
        up = 2.0 * jnp.floor(0.5 * log2(largest(v)) + 0.5)
        return v * jnp.exp2(-up), e + up

    def add(terms):
        top = terms[0][1]
        for _, e in terms[1:]:
            top = jnp.maximum(top, e)
        value = None
        for m, e in terms:
            part = m * jnp.exp2(e - top)
            value = part if value is None else value + part
        return value, top

    def post(m, value, e):
        outbox[m, :B, :] = value
        outbox[m, B:, :] = jnp.broadcast_to(0.5 * e, (AUX, B)).astype(BF16)
        send(m)

    def take(m, far):
        i = SENDS.index((m, far))
        box_copy(i).wait_recv()
        there = jnp.logical_and(q - far >= 0, q - far < NQ)
        value = jnp.where(there, inbox[i, :B, :].astype(F32), 0.0)
        return value, inbox[i, B:, :].astype(F32)[:1, :1]

    def take_scaled(m, far):
        value, e = take(m, far)
        return value, 2.0 * e

    def size(m, e):
        return log2(total(m * m)) + 2.0 * e

    x = outbox[0, :B, :]
    xx = twice(x)
    start_l, rank_l = take(0, 1)
    start_r, rank_r = take(0, -1)
    hop = 0.5 * (start_l + start_r)
    acc = None
    for group in GROUPS:
        for p in group:
            for w in ORDER[2 * p:2 * p + 2]:
                pltpu.make_async_copy(recv.at[w], recv.at[w], recv_sem.at[w]).wait()
        part = pairs(xx, group)
        acc = part if acc is None else acc + part
    m1, l1 = norm(mask * (acc + hop), jnp.zeros((1, 1), F32))
    x1 = m1.astype(BF16)
    post(1, x1, l1)
    mp, lp = norm(apply(x1), l1)
    post(2, mp.astype(BF16), lp)
    sizes = [size(m1, l1)]
    half = 0.5 * mask
    half_l = jnp.where(larger < rank_l, 0.5, 0.0).astype(F32)
    half_r = jnp.where(larger < rank_r, 0.5, 0.0).astype(F32)
    m1_l, l1_l = take_scaled(1, 1)
    m1_r, l1_r = take_scaled(1, -1)
    m2, l2 = norm(*add([(mp, lp), (half * m1_l, l1_l), (half * m1_r, l1_r)]))
    r, lr = norm(apply(m2.astype(BF16)), l2)
    sizes.append(size(m2, l2))
    m1_ll, l1_ll = take_scaled(1, 2)
    m1_rr, l1_rr = take_scaled(1, -2)
    mp_l, lp_l = take_scaled(2, 1)
    mp_r, lp_r = take_scaled(2, -1)
    m2_l, l2_l = add([(mp_l, lp_l), (half_l * m1, l1), (half_l * m1_ll, l1_ll)])
    m2_r, l2_r = add([(mp_r, lp_r), (half_r * m1, l1), (half_r * m1_rr, l1_rr)])
    m2_l = jnp.where(q > 0, m2_l, 0.0)
    m2_r = jnp.where(q < NQ - 1, m2_r, 0.0)
    m3, l3 = norm(*add([(r, lr), (half * m2_l, l2_l), (half * m2_r, l2_r)]))
    x3 = m3.astype(BF16)
    post(3, x3, l3)
    v, lv = norm(apply(x3), l3)
    sizes.append(size(m3, l3))
    for t in range(B // ROWS):
        rows = recv[:, t * ROWS:(t + 1) * ROWS, :].reshape(KR, B)
        env_out[:, t * ROWS:(t + 1) * ROWS, :] = dot(big, rows).astype(BF16).reshape(WM, ROWS, B)
    m3_l, l3_l = take_scaled(3, 1)
    m3_r, l3_r = take_scaled(3, -1)
    m4, l4 = norm(*add([(v, lv), (half * m3_l, l3_l), (half * m3_r, l3_r)]))
    sizes.append(size(m4, l4))

    lane = lax.broadcasted_iota(jnp.int32, (1, B), 1)
    line = jnp.full((1, B), -1e30, F32)
    for k in range(ITERS):
        line = jnp.where(lane == k, sizes[k] + ((ITERS - 1 - k) * LOG_EPS - LOG_N), line)
    psend[...] = line
    pall[q] = line

    def sum_copy(i):
        return pltpu.make_async_remote_copy(
            src_ref=psend, dst_ref=pall.at[q], send_sem=psem, recv_sem=precv,
            device_id=(g, lax.rem(q + i, NQ)), device_id_type=MESH,
        )

    def start_sum(i, carry):
        sum_copy(i).start()
        return carry

    lax.fori_loop(1, NQ, start_sum, 0)

    def drain(s, carry):
        for j in range(SLOTS):
            def body(j=j):
                for c in halo_copies(s, j):
                    c.wait_send()

                @pl.when(g != s + 1)
                def _():
                    deliver(s + 1, j).wait_send()

            each_slot(j, body)

        @pl.when(forwards(s))
        def _():
            forward(s).wait_send()

        return carry

    lax.fori_loop(0, STEPS, drain, 0)
    each_trans(lambda c: c.wait_send())

    @pl.when(g < STEPS)
    def _():
        for i in range(1, NS):
            mix_copy(i).wait_send()

    for i in range(len(SENDS)):
        box_copy(i).wait_send()
    others = pall.at[pl.ds(0, NQ - 1)]
    pltpu.make_async_copy(others, others, psem).wait()
    pltpu.make_async_copy(others, others, precv).wait()
    logs = pall[...].reshape(NQ, B)
    top = jnp.max(jnp.max(logs, axis=0, keepdims=True), axis=1, keepdims=True)
    top = jnp.maximum(top, ITERS * LOG_EPS)
    square = total(jnp.exp2(logs - top)) + jnp.exp2(ITERS * LOG_EPS - top)
    state[...] = m4 * (jnp.exp2(l4 - 0.5 * top) * lax.rsqrt(square))


def per_device(env_left, transfer, mpo_mix, right_env, start_state, block_rank):
    dma = pltpu.SemaphoreType.DMA
    vmem = pl.BlockSpec(memory_space=pltpu.VMEM)
    hbm = pl.BlockSpec(memory_space=pltpu.HBM)
    state, env = pl.pallas_call(
        kernel,
        out_shape=(
            jax.ShapeDtypeStruct((B, B), F32),
            jax.ShapeDtypeStruct((WM, B, B), BF16),
        ),
        in_specs=[hbm, hbm, hbm, hbm, hbm, pl.BlockSpec(memory_space=pltpu.SMEM)],
        out_specs=(vmem, vmem),
        scratch_shapes=[
            pltpu.VMEM((NS, SLOTS, B, B), BF16),
            pltpu.VMEM((STEPS, SLOTS, B, B), BF16),
            pltpu.VMEM((STEPS, SLOTS, B, B), BF16),
            pltpu.VMEM((WM, B, B), BF16),
            pltpu.VMEM((WM, B, B), BF16),
            pltpu.VMEM((PAIRS, 2 * B, B), BF16),
            pltpu.VMEM((NS, 3 * B, B), BF16),
            pltpu.VMEM((3, B, B), BF16),
            pltpu.VMEM((NS, 32, B), F32),
            pltpu.VMEM((32, B), F32),
            pltpu.VMEM((WM, 1, WM), F32),
            pltpu.VMEM((32, B), F32),
            pltpu.VMEM((B, B), F32),
            pltpu.VMEM((4, MSG, B), BF16),
            pltpu.VMEM((len(SENDS), MSG, B), BF16),
            pltpu.VMEM((1, B), F32),
            pltpu.VMEM((NQ, 1, B), F32),
            dma((SLOTS,)),
            dma((4,)),
            dma((WM,)),
            dma((NS, SLOTS)),
            dma((STEPS, 2, SLOTS)),
            dma((STEPS, 2, SLOTS)),
            dma((NS,)),
            dma((NS,)),
            dma((NS,)),
            dma((NS,)),
            dma((NS,)),
            dma((len(SENDS),)),
            dma((len(SENDS),)),
            dma,
            dma,
        ],
        compiler_params=pltpu.CompilerParams(
            collective_id=0, has_side_effects=True, vmem_limit_bytes=40 * 1024 * 1024
        ),
    )(
        *(
            pltpu.with_memory_space_constraint(value, pltpu.HBM)
            for value in (
                env_left.reshape(WM, B, B),
                transfer.reshape(3 * B, B),
                jnp.transpose(mpo_mix, (1, 0, 2)),
                right_env.reshape(WM, B, B),
                start_state.reshape(B, B),
            )
        ),
        block_rank,
    )
    return state.reshape(1, 1, B, B), env.reshape(1, WM, 1, B, B)


def solution(mesh):
    in_specs = (
        P(None, "blk", None, None),
        P("sec", "blk", None, None, None),
        P("sec", None, None),
        P("sec", None, "blk", None, None),
        P("sec", "blk", None, None),
        P("blk"),
    )
    out_specs = (P("sec", "blk", None, None), P("sec", None, "blk", None, None))
    return jax.shard_map(
        per_device, mesh=mesh, in_specs=in_specs, out_specs=out_specs, check_vma=False
    )
```

```python
import jax
import jax.numpy as jnp
from jax import lax
from jax.experimental import pallas as pl
from jax.experimental.pallas import tpu as pltpu
from jax.sharding import PartitionSpec as P

ITERS = 4
B = 128
WM = 26
NS = 8
NQ = 32
NX = 4
SLOTS = 4
STEPS = NS - 1
PAIRS = WM // 2
ROWS = 16
KR = WM * ROWS
FIRSTS = (0, 4, 7, 11, 14, 17, 20, 23)
ORDER = [f + j for j in range(3) for f in FIRSTS] + [3, 10]
GROUPS = (range(0, 4), range(4, 8), range(8, 13))
AUX = 16
MSG = B + AUX
SENDS = ((0, 1), (0, -1), (1, 1), (1, -1), (1, 2), (1, -2), (2, 1), (2, -1), (3, 1), (3, -1))
LOG_EPS = -19.931568569324174
LOG_N = 19.0
MESH = pl.DeviceIdType.MESH
F32 = jnp.float32
BF16 = jnp.bfloat16


def dot(a, b):
    return jnp.dot(a, b, preferred_element_type=F32)


def kernel(
    env_hbm, trans_hbm, mix_hbm, renv_hbm, start_hbm, rank, state, env_out,
    raw, halo, halo2, fart, ft, recv, renv, renvp, tall, tt, mixall, amat, mix_in, own_mix,
    start, outbox, inbox, psend, pall,
    load_sem, in_sem, recv_sem, deliver_sem,
    hrecv, hsend, h2recv, h2send, ftrecv, ftsend, trecv, tsend, fsend, mrecv, msend,
    xrecv, xsem, precv, psem,
):
    g = lax.axis_index("sec")
    q = lax.axis_index("blk")
    y = g // 2
    core = lax.rem(g, 2)
    right = lax.rem(q + 1, NQ)
    left = lax.rem(q + NQ - 1, NQ)
    first = 3 * g + jnp.where(g >= 1, 1, 0) + jnp.where(g >= 3, 1, 0)
    four = jnp.logical_or(g == 0, g == 2)
    x_at = lax.rem(q, NX)
    far = jnp.logical_or(x_at == 0, x_at == NX - 1)
    side = jnp.where(x_at == 0, 0, 1)
    beyond = jnp.where(x_at == 0, left, right)
    two_off = lax.rem(jnp.where(x_at == 2, q + 2, q + (NQ - 2)), NQ)

    loads = [
        pltpu.make_async_copy(trans_hbm, tall.at[g], in_sem.at[0]),
        pltpu.make_async_copy(mix_hbm, mix_in, in_sem.at[1]),
        pltpu.make_async_copy(start_hbm, start, in_sem.at[2]),
        pltpu.make_async_copy(renv_hbm, renv, in_sem.at[3]),
    ]

    def each_slot(j, body):
        if j < SLOTS - 1:
            body()
        else:
            pl.when(four)(body)

    def load(j):
        return pltpu.make_async_copy(env_hbm.at[first + j], raw.at[0, j], load_sem.at[j])

    loads[0].start()
    for j in range(SLOTS):
        each_slot(j, lambda j=j: load(j).start())
    for c in loads[1:]:
        c.start()

    barrier = pltpu.get_barrier_semaphore()

    def greet_sec(i, carry):
        pl.semaphore_signal(barrier, inc=1, device_id=(lax.rem(g + i, NS), q), device_id_type=MESH)
        return carry

    def greet_blk(i, carry):
        pl.semaphore_signal(barrier, inc=1, device_id=(g, lax.rem(q + i, NQ)), device_id_type=MESH)
        return carry

    lax.fori_loop(1, NS, greet_sec, 0)
    lax.fori_loop(1, NQ, greet_blk, 0)

    @pl.when(jnp.logical_and(far, core == 0))
    def _():
        pl.semaphore_signal(barrier, inc=1, device_id=(g + 1, beyond), device_id_type=MESH)


    @pl.when(g == 0)
    def _():
        def body(w, carry):
            pltpu.make_async_copy(env_hbm.at[w], recv.at[w], recv_sem.at[w]).start()
            return carry

        lax.fori_loop(0, WM, body, 0)

    own_mix[...] = jnp.zeros_like(own_mix)
    loads[1].wait()
    own_mix[:WM, :WM] = mix_in[...].reshape(WM, WM)
    mixall[g] = own_mix[...]
    row = lax.broadcasted_iota(jnp.int32, (32, B), 0)
    col = lax.broadcasted_iota(jnp.int32, (32, B), 1)
    amat[...] = jnp.where(row == col, 1.0, 0.0).astype(F32)
    keep0 = lax.broadcasted_iota(jnp.int32, (B, B), 0)
    keep1 = lax.broadcasted_iota(jnp.int32, (B, B), 1)
    larger = jnp.maximum(keep0, keep1).astype(F32)
    my_rank = rank[0].astype(F32)
    mask = jnp.where(larger < my_rank, 1.0, 0.0).astype(F32)
    loads[2].wait()
    outbox[0, :B, :] = (start[...] * mask).astype(BF16)
    outbox[0, B:, :] = jnp.full((AUX, B), my_rank, F32).astype(BF16)
    loads[0].wait()
    for j in range(SLOTS):
        each_slot(j, lambda j=j: load(j).wait())

    pl.semaphore_wait(barrier, NS - 1 + NQ - 1 + jnp.where(jnp.logical_and(far, core == 1), 1, 0))

    def crossed(s):
        return jnp.logical_or(s == 0, lax.rem(s, 2) == 1)

    def halo_copy(s, j, to):
        return pltpu.make_async_remote_copy(
            src_ref=raw.at[s, j], dst_ref=halo.at[s, 1 - to, j],
            send_sem=hsend.at[s, to, j], recv_sem=hrecv.at[s, 1 - to, j],
            device_id=(g, right if to else left), device_id_type=MESH,
        )

    def inside(to):
        return x_at != (NX - 1 if to else 0)

    def each_halo(s, j, act):
        for to in range(2):
            pl.when(jnp.logical_or(inside(to), crossed(s)))(lambda to=to: act(halo_copy(s, j, to)))

    def wait_halo(s, j):
        for at in range(2):
            @pl.when(jnp.logical_or(inside(at), crossed(s)))
            def _():
                halo_copy(s, j, 1 - at).wait_recv()

    def halo2_copy(s, j):
        return pltpu.make_async_remote_copy(
            src_ref=raw.at[s, j], dst_ref=halo2.at[s // 2, j],
            send_sem=h2send.at[s // 2, j], recv_sem=h2recv.at[s // 2, j],
            device_id=(g, two_off), device_id_type=MESH,
        )

    def each_halo2(s, j, act):
        pl.when(jnp.logical_and(jnp.logical_not(far), lax.rem(s, 2) == 1))(lambda: act(halo2_copy(s, j)))

    def start_halo(s, j):
        each_halo(s, j, lambda c: c.start())
        each_halo2(s, j, lambda c: c.start())

    def far_trans(s, i):
        return pltpu.make_async_remote_copy(
            src_ref=tall.at[s], dst_ref=fart.at[s // 2],
            send_sem=ftsend.at[s // 2, i], recv_sem=ftrecv.at[s // 2],
            device_id=(g - i, beyond), device_id_type=MESH,
        )

    def each_far_trans(s, act):
        @pl.when(jnp.logical_and(jnp.logical_and(far, core == 1), jnp.logical_and(lax.rem(s, 2) == 1, s < STEPS)))
        def _():
            for i in range(2):
                act(far_trans(s, i))

    def trans_copy(src, s, sem, other):
        return pltpu.make_async_remote_copy(
            src_ref=src, dst_ref=tall.at[s], send_sem=sem, recv_sem=trecv.at[s],
            device_id=(other, q), device_id_type=MESH,
        )

    def mix_copy(i):
        return pltpu.make_async_remote_copy(
            src_ref=own_mix, dst_ref=mixall.at[g], send_sem=msend.at[i], recv_sem=mrecv.at[g],
            device_id=(lax.rem(g + i, NS), q), device_id_type=MESH,
        )

    def each_trans(act):
        @pl.when(g == 0)
        def _():
            for i in range(1, NS):
                act(trans_copy(tall.at[g], 0, tsend.at[i], i))

        @pl.when(jnp.logical_and(g > 0, g < STEPS))
        def _():
            act(trans_copy(tall.at[g], g, tsend.at[0], g + 1 - 2 * core))
            for i in range(1, 4):
                act(trans_copy(tall.at[g], g, tsend.at[i], lax.rem(g + 2 * i, NS)))

    for j in range(SLOTS):
        each_slot(j, lambda j=j: start_halo(0, j))
    each_trans(lambda c: c.start())

    @pl.when(g < STEPS)
    def _():
        for i in range(1, NS):
            mix_copy(i).start()

    def box_copy(i):
        m, far = SENDS[i]
        return pltpu.make_async_remote_copy(
            src_ref=outbox.at[m], dst_ref=inbox.at[i], send_sem=xsem.at[i], recv_sem=xrecv.at[i],
            device_id=(g, lax.rem(q + (NQ + far), NQ)), device_id_type=MESH,
        )

    def send(m):
        for i in range(len(SENDS)):
            if SENDS[i][0] == m:
                box_copy(i).start()

    send(0)

    def deliver(s, j):
        return pltpu.make_async_remote_copy(
            src_ref=raw.at[s, j], dst_ref=recv.at[first + j],
            send_sem=deliver_sem.at[s, j], recv_sem=recv_sem.at[first + j],
            device_id=(s, q), device_id_type=MESH,
        )

    def deliver_local(s, j):
        return pltpu.make_async_copy(raw.at[s, j], recv.at[first + j], recv_sem.at[first + j])

    def forwards(s):
        return jnp.logical_and(
            jnp.logical_and(core == lax.rem(s, 2), y != s // 2), jnp.logical_and(s >= 1, s < STEPS)
        )

    def forward(s):
        return trans_copy(tall.at[s], s, fsend.at[s], g + 1 - 2 * core)

    def wait_trans(s):
        pltpu.make_async_copy(tall.at[s], tall.at[s], trecv.at[s]).wait()

    def pass_on(s):
        @pl.when(forwards(s))
        def _():
            wait_trans(s)
            forward(s).start()

        each_far_trans(s, lambda c: c.start())

    pass_on(1)

    def step(s, carry):
        @pl.when(jnp.logical_and(g != s, jnp.logical_not(forwards(s))))
        def _():
            wait_trans(s)

        pass_on(s + 2)
        redo = jnp.logical_and(far, lax.rem(s, 2) == 1)

        for d in range(3):
            t = tall[s, d * B:(d + 1) * B, :].T
            if d == 0:
                t = jnp.where(q > 0, t, jnp.zeros_like(t))
            if d == 2:
                t = jnp.where(q < NQ - 1, t, jnp.zeros_like(t))
            tt[d] = t

        def carry_on(parts, turned, tensor):
            parts = [dot(turned[d], parts[d]).astype(BF16) for d in range(3)]
            return dot(jnp.concatenate(parts, axis=1), tensor).astype(BF16)

        for j in range(SLOTS):
            def body(j=j):
                wait_halo(s, j)
                raw[s + 1, j] = carry_on([halo[s, 0, j], raw[s, j], halo[s, 1, j]], tt, tall[s])

                @pl.when(s < STEPS - 1)
                def _():
                    start_halo(s + 1, j)

                @pl.when(g != s + 1)
                def _():
                    deliver(s + 1, j).start()

                @pl.when(g == s + 1)
                def _():
                    deliver_local(s + 1, j).start()

            each_slot(j, body)

        @pl.when(redo)
        def _():
            pltpu.make_async_copy(fart.at[s // 2], fart.at[s // 2], ftrecv.at[s // 2]).wait()
            for d in range(3):
                ft[d] = fart[s // 2, d * B:(d + 1) * B, :].T
            for j in range(SLOTS):
                def again(j=j):
                    halo2_copy(s, j).wait_recv()
                    mine, other = raw[s, j], halo2[s // 2, j]
                    low = jnp.where(x_at == 0, other, mine)
                    high = jnp.where(x_at == 0, mine, other)
                    halo[s + 1, side, j] = carry_on([low, halo[s, side, j], high], ft, fart[s // 2])

                each_slot(j, again)

        @pl.when(g != s)
        def _():
            pltpu.make_async_copy(mixall.at[s], mixall.at[s], mrecv.at[s]).wait()

        @pl.when(s < g)
        def _():
            amat[...] = jnp.dot(mixall[s][:, :32], amat[...], precision=lax.Precision.HIGHEST, preferred_element_type=F32)

        return carry

    lax.fori_loop(0, STEPS, step, 0)

    a = amat[...][:, :32].astype(BF16)
    wide = lax.broadcasted_iota(jnp.int32, (KR, 32), 0) // ROWS
    spread = jnp.where(wide == lax.broadcasted_iota(jnp.int32, (KR, 32), 1), 1.0, 0.0).astype(BF16)
    r0 = lax.rem(lax.broadcasted_iota(jnp.int32, (KR, KR), 0), ROWS)
    r1 = lax.rem(lax.broadcasted_iota(jnp.int32, (KR, KR), 1), ROWS)

    def widen(half):
        full = lax.dot_general(half.astype(BF16), spread, (((1,), (1,)), ((), ())), preferred_element_type=F32)
        return jnp.where(r0 == r1, full, 0.0).astype(BF16)

    turned = widen(lax.dot_general(spread, a, (((1,), (1,)), ((), ())), preferred_element_type=F32))
    loads[3].wait()
    for t in range(B // ROWS):
        rows = renv[:, t * ROWS:(t + 1) * ROWS, :].reshape(KR, B)
        mixed = dot(turned, rows).astype(BF16).reshape(WM, ROWS, B)
        for i, w in enumerate(ORDER):
            at = (i % 2) * B + t * ROWS
            renvp[i // 2, at:at + ROWS, :] = mixed[w]
    big = widen(dot(spread, a))

    def pairs(xx, group):
        acc = None
        for p in group:
            pair = jnp.concatenate([recv[ORDER[2 * p]], recv[ORDER[2 * p + 1]]], axis=1)
            term = dot(dot(pair, xx).astype(BF16), renvp[p])
            acc = term if acc is None else acc + term
        return acc

    def twice(x):
        zero = jnp.zeros_like(x)
        return jnp.concatenate([jnp.concatenate([x, zero], axis=1), jnp.concatenate([zero, x], axis=1)], axis=0)

    def apply(x):
        return pairs(twice(x), range(PAIRS)) * mask

    def largest(v):
        return jnp.max(jnp.max(jnp.abs(v), axis=0, keepdims=True), axis=1, keepdims=True)

    def total(v):
        return jnp.sum(jnp.sum(v, axis=0, keepdims=True), axis=1, keepdims=True)

    def log2(v):
        return jnp.log(jnp.maximum(v, 1e-30)) * 1.4426950408889634

    def norm(v, e):
        up = 2.0 * jnp.floor(0.5 * log2(largest(v)) + 0.5)
        return v * jnp.exp2(-up), e + up

    def add(terms):
        top = terms[0][1]
        for _, e in terms[1:]:
            top = jnp.maximum(top, e)
        value = None
        for m, e in terms:
            part = m * jnp.exp2(e - top)
            value = part if value is None else value + part
        return value, top

    def post(m, value, e):
        outbox[m, :B, :] = value
        outbox[m, B:, :] = jnp.broadcast_to(0.5 * e, (AUX, B)).astype(BF16)
        send(m)

    def take(m, far):
        i = SENDS.index((m, far))
        box_copy(i).wait_recv()
        there = jnp.logical_and(q - far >= 0, q - far < NQ)
        value = jnp.where(there, inbox[i, :B, :].astype(F32), 0.0)
        return value, inbox[i, B:, :].astype(F32)[:1, :1]

    def take_scaled(m, far):
        value, e = take(m, far)
        return value, 2.0 * e

    def size(m, e):
        return log2(total(m * m)) + 2.0 * e

    x = outbox[0, :B, :]
    xx = twice(x)
    start_l, rank_l = take(0, 1)
    start_r, rank_r = take(0, -1)
    hop = 0.5 * (start_l + start_r)
    acc = None
    for group in GROUPS:
        for p in group:
            for w in ORDER[2 * p:2 * p + 2]:
                pltpu.make_async_copy(recv.at[w], recv.at[w], recv_sem.at[w]).wait()
        part = pairs(xx, group)
        acc = part if acc is None else acc + part
    m1, l1 = norm(mask * (acc + hop), jnp.zeros((1, 1), F32))
    x1 = m1.astype(BF16)
    post(1, x1, l1)
    mp, lp = norm(apply(x1), l1)
    post(2, mp.astype(BF16), lp)
    sizes = [size(m1, l1)]
    half = 0.5 * mask
    half_l = jnp.where(larger < rank_l, 0.5, 0.0).astype(F32)
    half_r = jnp.where(larger < rank_r, 0.5, 0.0).astype(F32)
    m1_l, l1_l = take_scaled(1, 1)
    m1_r, l1_r = take_scaled(1, -1)
    m2, l2 = norm(*add([(mp, lp), (half * m1_l, l1_l), (half * m1_r, l1_r)]))
    r, lr = norm(apply(m2.astype(BF16)), l2)
    sizes.append(size(m2, l2))
    m1_ll, l1_ll = take_scaled(1, 2)
    m1_rr, l1_rr = take_scaled(1, -2)
    mp_l, lp_l = take_scaled(2, 1)
    mp_r, lp_r = take_scaled(2, -1)
    m2_l, l2_l = add([(mp_l, lp_l), (half_l * m1, l1), (half_l * m1_ll, l1_ll)])
    m2_r, l2_r = add([(mp_r, lp_r), (half_r * m1, l1), (half_r * m1_rr, l1_rr)])
    m2_l = jnp.where(q > 0, m2_l, 0.0)
    m2_r = jnp.where(q < NQ - 1, m2_r, 0.0)
    m3, l3 = norm(*add([(r, lr), (half * m2_l, l2_l), (half * m2_r, l2_r)]))
    x3 = m3.astype(BF16)
    post(3, x3, l3)
    v, lv = norm(apply(x3), l3)
    sizes.append(size(m3, l3))
    for t in range(B // ROWS):
        rows = recv[:, t * ROWS:(t + 1) * ROWS, :].reshape(KR, B)
        env_out[:, t * ROWS:(t + 1) * ROWS, :] = dot(big, rows).astype(BF16).reshape(WM, ROWS, B)
    m3_l, l3_l = take_scaled(3, 1)
    m3_r, l3_r = take_scaled(3, -1)
    m4, l4 = norm(*add([(v, lv), (half * m3_l, l3_l), (half * m3_r, l3_r)]))
    sizes.append(size(m4, l4))

    lane = lax.broadcasted_iota(jnp.int32, (1, B), 1)
    line = jnp.full((1, B), -1e30, F32)
    for k in range(ITERS):
        line = jnp.where(lane == k, sizes[k] + ((ITERS - 1 - k) * LOG_EPS - LOG_N), line)
    psend[...] = line
    pall[q] = line

    def sum_copy(i):
        return pltpu.make_async_remote_copy(
            src_ref=psend, dst_ref=pall.at[q], send_sem=psem, recv_sem=precv,
            device_id=(g, lax.rem(q + i, NQ)), device_id_type=MESH,
        )

    def start_sum(i, carry):
        sum_copy(i).start()
        return carry

    lax.fori_loop(1, NQ, start_sum, 0)

    def drain(s, carry):
        for j in range(SLOTS):
            def body(j=j):
                each_halo(s, j, lambda c: c.wait_send())
                each_halo2(s, j, lambda c: c.wait_send())

                @pl.when(g != s + 1)
                def _():
                    deliver(s + 1, j).wait_send()

            each_slot(j, body)

        @pl.when(forwards(s))
        def _():
            forward(s).wait_send()

        each_far_trans(s, lambda c: c.wait_send())
        return carry

    lax.fori_loop(0, STEPS, drain, 0)
    each_trans(lambda c: c.wait_send())

    @pl.when(g < STEPS)
    def _():
        for i in range(1, NS):
            mix_copy(i).wait_send()

    for i in range(len(SENDS)):
        box_copy(i).wait_send()
    others = pall.at[pl.ds(0, NQ - 1)]
    pltpu.make_async_copy(others, others, psem).wait()
    pltpu.make_async_copy(others, others, precv).wait()
    logs = pall[...].reshape(NQ, B)
    top = jnp.max(jnp.max(logs, axis=0, keepdims=True), axis=1, keepdims=True)
    top = jnp.maximum(top, ITERS * LOG_EPS)
    square = total(jnp.exp2(logs - top)) + jnp.exp2(ITERS * LOG_EPS - top)
    state[...] = m4 * (jnp.exp2(l4 - 0.5 * top) * lax.rsqrt(square))


def per_device(env_left, transfer, mpo_mix, right_env, start_state, block_rank):
    dma = pltpu.SemaphoreType.DMA
    vmem = pl.BlockSpec(memory_space=pltpu.VMEM)
    hbm = pl.BlockSpec(memory_space=pltpu.HBM)
    state, env = pl.pallas_call(
        kernel,
        out_shape=(
            jax.ShapeDtypeStruct((B, B), F32),
            jax.ShapeDtypeStruct((WM, B, B), BF16),
        ),
        in_specs=[hbm, hbm, hbm, hbm, hbm, pl.BlockSpec(memory_space=pltpu.SMEM)],
        out_specs=(vmem, vmem),
        scratch_shapes=[
            pltpu.VMEM((NS, SLOTS, B, B), BF16),
            pltpu.VMEM((STEPS, 2, SLOTS, B, B), BF16),
            pltpu.VMEM((3, SLOTS, B, B), BF16),
            pltpu.VMEM((3, 3 * B, B), BF16),
            pltpu.VMEM((3, B, B), BF16),
            pltpu.VMEM((WM, B, B), BF16),
            pltpu.VMEM((WM, B, B), BF16),
            pltpu.VMEM((PAIRS, 2 * B, B), BF16),
            pltpu.VMEM((NS, 3 * B, B), BF16),
            pltpu.VMEM((3, B, B), BF16),
            pltpu.VMEM((NS, 32, B), F32),
            pltpu.VMEM((32, B), F32),
            pltpu.VMEM((WM, 1, WM), F32),
            pltpu.VMEM((32, B), F32),
            pltpu.VMEM((B, B), F32),
            pltpu.VMEM((4, MSG, B), BF16),
            pltpu.VMEM((len(SENDS), MSG, B), BF16),
            pltpu.VMEM((1, B), F32),
            pltpu.VMEM((NQ, 1, B), F32),
            dma((SLOTS,)),
            dma((4,)),
            dma((WM,)),
            dma((NS, SLOTS)),
            dma((STEPS, 2, SLOTS)),
            dma((STEPS, 2, SLOTS)),
            dma((3, SLOTS)),
            dma((3, SLOTS)),
            dma((3,)),
            dma((3, 2)),
            dma((NS,)),
            dma((NS,)),
            dma((NS,)),
            dma((NS,)),
            dma((NS,)),
            dma((len(SENDS),)),
            dma((len(SENDS),)),
            dma,
            dma,
        ],
        compiler_params=pltpu.CompilerParams(
            collective_id=0, has_side_effects=True, vmem_limit_bytes=40 * 1024 * 1024
        ),
    )(
        *(
            pltpu.with_memory_space_constraint(value, pltpu.HBM)
            for value in (
                env_left.reshape(WM, B, B),
                transfer.reshape(3 * B, B),
                jnp.transpose(mpo_mix, (1, 0, 2)),
                right_env.reshape(WM, B, B),
                start_state.reshape(B, B),
            )
        ),
        block_rank,
    )
    return state.reshape(1, 1, B, B), env.reshape(1, WM, 1, B, B)


def solution(mesh):
    in_specs = (
        P(None, "blk", None, None),
        P("sec", "blk", None, None, None),
        P("sec", None, None),
        P("sec", None, "blk", None, None),
        P("sec", "blk", None, None),
        P("blk"),
    )
    out_specs = (P("sec", "blk", None, None), P("sec", None, "blk", None, None))
    return jax.shard_map(
        per_device, mesh=mesh, in_specs=in_specs, out_specs=out_specs, check_vma=False
    )
```

```python
import jax
import jax.numpy as jnp
from jax import lax
from jax.experimental import pallas as pl
from jax.experimental.pallas import tpu as pltpu
from jax.sharding import PartitionSpec as P

ITERS = 4
B = 128
WM = 26
NS = 8
NQ = 32
NX = 4
NEAR = (1, NQ - 1, 2, NQ - 2)
SLOTS = 4
STEPS = NS - 1
PAIRS = WM // 2
ROWS = 16
KR = WM * ROWS
FIRSTS = (0, 4, 7, 11, 14, 17, 20, 23)
ORDER = [f + j for j in range(3) for f in FIRSTS] + [3, 10]
GROUPS = (range(0, 4), range(4, 8), range(8, 13))
AUX = 16
MSG = B + AUX
SENDS = ((0, 1), (0, -1), (1, 1), (1, -1), (1, 2), (1, -2), (2, 1), (2, -1), (3, 1), (3, -1))
LOG_EPS = -19.931568569324174
LOG_N = 19.0
MESH = pl.DeviceIdType.MESH
F32 = jnp.float32
BF16 = jnp.bfloat16


def dot(a, b):
    return jnp.dot(a, b, preferred_element_type=F32)


def kernel(
    env_hbm, trans_hbm, mix_hbm, renv_hbm, start_hbm, rank, state, env_out,
    raw, halo, halo2, fart, ft, recv, renv, renvp, tall, tt, mixall, amat, mix_in, own_mix,
    start, outbox, inbox, psend, pall,
    load_sem, in_sem, recv_sem, deliver_sem,
    hrecv, hsend, h2recv, h2send, ftrecv, ftsend, trecv, tsend, fsend, mrecv, msend,
    xrecv, xsem, precv, psem, known,
):
    g = lax.axis_index("sec")
    q = lax.axis_index("blk")
    y = g // 2
    core = lax.rem(g, 2)
    right = lax.rem(q + 1, NQ)
    left = lax.rem(q + NQ - 1, NQ)
    first = 3 * g + jnp.where(g >= 1, 1, 0) + jnp.where(g >= 3, 1, 0)
    four = jnp.logical_or(g == 0, g == 2)
    x_at = lax.rem(q, NX)
    far = jnp.logical_or(x_at == 0, x_at == NX - 1)
    side = jnp.where(x_at == 0, 0, 1)
    beyond = jnp.where(x_at == 0, left, right)
    two_off = lax.rem(jnp.where(x_at == 2, q + 2, q + (NQ - 2)), NQ)

    barrier = pltpu.get_barrier_semaphore()

    def greet_sec(i, carry):
        pl.semaphore_signal(barrier, inc=1, device_id=(lax.rem(g + i, NS), q), device_id_type=MESH)
        return carry

    lax.fori_loop(1, NS, greet_sec, 0)
    for i in NEAR:
        pl.semaphore_signal(barrier, inc=1, device_id=(g, lax.rem(q + i, NQ)), device_id_type=MESH)

    @pl.when(jnp.logical_and(far, core == 0))
    def _():
        pl.semaphore_signal(barrier, inc=1, device_id=(g + 1, beyond), device_id_type=MESH)


    loads = [
        pltpu.make_async_copy(trans_hbm, tall.at[g], in_sem.at[0]),
        pltpu.make_async_copy(mix_hbm, mix_in, in_sem.at[1]),
        pltpu.make_async_copy(start_hbm, start, in_sem.at[2]),
        pltpu.make_async_copy(renv_hbm, renv, in_sem.at[3]),
    ]

    def each_slot(j, body):
        if j < SLOTS - 1:
            body()
        else:
            pl.when(four)(body)

    def load(j):
        return pltpu.make_async_copy(env_hbm.at[first + j], raw.at[0, j], load_sem.at[j])

    loads[0].start()
    for j in range(SLOTS):
        each_slot(j, lambda j=j: load(j).start())
    for c in loads[1:]:
        c.start()

    @pl.when(g == 0)
    def _():
        def body(w, carry):
            pltpu.make_async_copy(env_hbm.at[w], recv.at[w], recv_sem.at[w]).start()
            return carry

        lax.fori_loop(0, WM, body, 0)

    own_mix[...] = jnp.zeros_like(own_mix)
    loads[1].wait()
    own_mix[:WM, :WM] = mix_in[...].reshape(WM, WM)
    mixall[g] = own_mix[...]
    row = lax.broadcasted_iota(jnp.int32, (32, B), 0)
    col = lax.broadcasted_iota(jnp.int32, (32, B), 1)
    amat[...] = jnp.where(row == col, 1.0, 0.0).astype(F32)
    keep0 = lax.broadcasted_iota(jnp.int32, (B, B), 0)
    keep1 = lax.broadcasted_iota(jnp.int32, (B, B), 1)
    larger = jnp.maximum(keep0, keep1).astype(F32)
    my_rank = rank[0].astype(F32)
    mask = jnp.where(larger < my_rank, 1.0, 0.0).astype(F32)
    loads[2].wait()
    outbox[0, :B, :] = (start[...] * mask).astype(BF16)
    outbox[0, B:, :] = jnp.full((AUX, B), my_rank, F32).astype(BF16)
    loads[0].wait()
    for j in range(SLOTS):
        each_slot(j, lambda j=j: load(j).wait())

    pl.semaphore_wait(barrier, NS - 1 + len(NEAR) + jnp.where(jnp.logical_and(far, core == 1), 1, 0))

    def crossed(s):
        return jnp.logical_or(s == 0, lax.rem(s, 2) == 1)

    def halo_copy(s, j, to):
        return pltpu.make_async_remote_copy(
            src_ref=raw.at[s, j], dst_ref=halo.at[s, 1 - to, j],
            send_sem=hsend.at[s, to, j], recv_sem=hrecv.at[s, 1 - to, j],
            device_id=(g, right if to else left), device_id_type=MESH,
        )

    def inside(to):
        return x_at != (NX - 1 if to else 0)

    def each_halo(s, j, act):
        for to in range(2):
            pl.when(jnp.logical_or(inside(to), crossed(s)))(lambda to=to: act(halo_copy(s, j, to)))

    def wait_halo(s, j):
        for at in range(2):
            @pl.when(jnp.logical_or(inside(at), crossed(s)))
            def _():
                halo_copy(s, j, 1 - at).wait_recv()

    def halo2_copy(s, j):
        return pltpu.make_async_remote_copy(
            src_ref=raw.at[s, j], dst_ref=halo2.at[s // 2, j],
            send_sem=h2send.at[s // 2, j], recv_sem=h2recv.at[s // 2, j],
            device_id=(g, two_off), device_id_type=MESH,
        )

    def each_halo2(s, j, act):
        pl.when(jnp.logical_and(jnp.logical_not(far), lax.rem(s, 2) == 1))(lambda: act(halo2_copy(s, j)))

    def start_halo(s, j):
        each_halo(s, j, lambda c: c.start())
        each_halo2(s, j, lambda c: c.start())

    def far_trans(s, i):
        return pltpu.make_async_remote_copy(
            src_ref=tall.at[s], dst_ref=fart.at[s // 2],
            send_sem=ftsend.at[s // 2, i], recv_sem=ftrecv.at[s // 2],
            device_id=(g - i, beyond), device_id_type=MESH,
        )

    def each_far_trans(s, act):
        @pl.when(jnp.logical_and(jnp.logical_and(far, core == 1), jnp.logical_and(lax.rem(s, 2) == 1, s < STEPS)))
        def _():
            for i in range(2):
                act(far_trans(s, i))

    def trans_copy(src, s, sem, other):
        return pltpu.make_async_remote_copy(
            src_ref=src, dst_ref=tall.at[s], send_sem=sem, recv_sem=trecv.at[s],
            device_id=(other, q), device_id_type=MESH,
        )

    def mix_copy(i):
        return pltpu.make_async_remote_copy(
            src_ref=own_mix, dst_ref=mixall.at[g], send_sem=msend.at[i], recv_sem=mrecv.at[g],
            device_id=(lax.rem(g + i, NS), q), device_id_type=MESH,
        )

    def each_trans(act):
        @pl.when(g == 0)
        def _():
            for i in range(1, NS):
                act(trans_copy(tall.at[g], 0, tsend.at[i], i))

        @pl.when(jnp.logical_and(g > 0, g < STEPS))
        def _():
            act(trans_copy(tall.at[g], g, tsend.at[0], g + 1 - 2 * core))
            for i in range(1, 4):
                act(trans_copy(tall.at[g], g, tsend.at[i], lax.rem(g + 2 * i, NS)))

    for j in range(SLOTS):
        each_slot(j, lambda j=j: start_halo(0, j))
    each_trans(lambda c: c.start())

    @pl.when(g < STEPS)
    def _():
        for i in range(1, NS):
            mix_copy(i).start()

    def box_copy(i):
        m, far = SENDS[i]
        return pltpu.make_async_remote_copy(
            src_ref=outbox.at[m], dst_ref=inbox.at[i], send_sem=xsem.at[i], recv_sem=xrecv.at[i],
            device_id=(g, lax.rem(q + (NQ + far), NQ)), device_id_type=MESH,
        )

    def send(m):
        for i in range(len(SENDS)):
            if SENDS[i][0] == m:
                box_copy(i).start()

    send(0)

    def deliver(s, j):
        return pltpu.make_async_remote_copy(
            src_ref=raw.at[s, j], dst_ref=recv.at[first + j],
            send_sem=deliver_sem.at[s, j], recv_sem=recv_sem.at[first + j],
            device_id=(s, q), device_id_type=MESH,
        )

    def deliver_local(s, j):
        return pltpu.make_async_copy(raw.at[s, j], recv.at[first + j], recv_sem.at[first + j])

    def forwards(s):
        return jnp.logical_and(
            jnp.logical_and(core == lax.rem(s, 2), y != s // 2), jnp.logical_and(s >= 1, s < STEPS)
        )

    def forward(s):
        return trans_copy(tall.at[s], s, fsend.at[s], g + 1 - 2 * core)

    def wait_trans(s):
        pltpu.make_async_copy(tall.at[s], tall.at[s], trecv.at[s]).wait()

    def pass_on(s):
        @pl.when(forwards(s))
        def _():
            wait_trans(s)
            forward(s).start()

        each_far_trans(s, lambda c: c.start())

    pass_on(1)

    def tell(i):
        far_off = 2 << i
        for other in (q + far_off, q + (NQ - far_off)):
            pl.semaphore_signal(known.at[i], inc=1, device_id=(g, lax.rem(other, NQ)), device_id_type=MESH)

    def heard(i):
        pl.semaphore_wait(known.at[i], 2)

    tell(0)

    def step(s, carry):
        for i in range(3):
            @pl.when(s == i + 1)
            def _():
                heard(i)
                if i < 2:
                    tell(i + 1)

        @pl.when(jnp.logical_and(g != s, jnp.logical_not(forwards(s))))
        def _():
            wait_trans(s)

        pass_on(s + 2)
        redo = jnp.logical_and(far, lax.rem(s, 2) == 1)

        for d in range(3):
            t = tall[s, d * B:(d + 1) * B, :].T
            if d == 0:
                t = jnp.where(q > 0, t, jnp.zeros_like(t))
            if d == 2:
                t = jnp.where(q < NQ - 1, t, jnp.zeros_like(t))
            tt[d] = t

        def carry_on(parts, turned, tensor):
            parts = [dot(turned[d], parts[d]).astype(BF16) for d in range(3)]
            return dot(jnp.concatenate(parts, axis=1), tensor).astype(BF16)

        for j in range(SLOTS):
            def body(j=j):
                wait_halo(s, j)
                raw[s + 1, j] = carry_on([halo[s, 0, j], raw[s, j], halo[s, 1, j]], tt, tall[s])

                @pl.when(s < STEPS - 1)
                def _():
                    start_halo(s + 1, j)

                @pl.when(g != s + 1)
                def _():
                    deliver(s + 1, j).start()

                @pl.when(g == s + 1)
                def _():
                    deliver_local(s + 1, j).start()

            each_slot(j, body)

        @pl.when(redo)
        def _():
            pltpu.make_async_copy(fart.at[s // 2], fart.at[s // 2], ftrecv.at[s // 2]).wait()
            for d in range(3):
                ft[d] = fart[s // 2, d * B:(d + 1) * B, :].T
            for j in range(SLOTS):
                def again(j=j):
                    halo2_copy(s, j).wait_recv()
                    mine, other = raw[s, j], halo2[s // 2, j]
                    low = jnp.where(x_at == 0, other, mine)
                    high = jnp.where(x_at == 0, mine, other)
                    halo[s + 1, side, j] = carry_on([low, halo[s, side, j], high], ft, fart[s // 2])

                each_slot(j, again)

        @pl.when(g != s)
        def _():
            pltpu.make_async_copy(mixall.at[s], mixall.at[s], mrecv.at[s]).wait()

        @pl.when(s < g)
        def _():
            amat[...] = jnp.dot(mixall[s][:, :32], amat[...], precision=lax.Precision.HIGHEST, preferred_element_type=F32)

        return carry

    lax.fori_loop(0, STEPS, step, 0)

    a = amat[...][:, :32].astype(BF16)
    wide = lax.broadcasted_iota(jnp.int32, (KR, 32), 0) // ROWS
    spread = jnp.where(wide == lax.broadcasted_iota(jnp.int32, (KR, 32), 1), 1.0, 0.0).astype(BF16)
    r0 = lax.rem(lax.broadcasted_iota(jnp.int32, (KR, KR), 0), ROWS)
    r1 = lax.rem(lax.broadcasted_iota(jnp.int32, (KR, KR), 1), ROWS)

    def widen(half):
        full = lax.dot_general(half.astype(BF16), spread, (((1,), (1,)), ((), ())), preferred_element_type=F32)
        return jnp.where(r0 == r1, full, 0.0).astype(BF16)

    turned = widen(lax.dot_general(spread, a, (((1,), (1,)), ((), ())), preferred_element_type=F32))
    loads[3].wait()
    for t in range(B // ROWS):
        rows = renv[:, t * ROWS:(t + 1) * ROWS, :].reshape(KR, B)
        mixed = dot(turned, rows).astype(BF16).reshape(WM, ROWS, B)
        for i, w in enumerate(ORDER):
            at = (i % 2) * B + t * ROWS
            renvp[i // 2, at:at + ROWS, :] = mixed[w]
    big = widen(dot(spread, a))

    def pairs(xx, group):
        acc = None
        for p in group:
            pair = jnp.concatenate([recv[ORDER[2 * p]], recv[ORDER[2 * p + 1]]], axis=1)
            term = dot(dot(pair, xx).astype(BF16), renvp[p])
            acc = term if acc is None else acc + term
        return acc

    def twice(x):
        zero = jnp.zeros_like(x)
        return jnp.concatenate([jnp.concatenate([x, zero], axis=1), jnp.concatenate([zero, x], axis=1)], axis=0)

    def apply(x):
        return pairs(twice(x), range(PAIRS)) * mask

    def largest(v):
        return jnp.max(jnp.max(jnp.abs(v), axis=0, keepdims=True), axis=1, keepdims=True)

    def total(v):
        return jnp.sum(jnp.sum(v, axis=0, keepdims=True), axis=1, keepdims=True)

    def log2(v):
        return jnp.log(jnp.maximum(v, 1e-30)) * 1.4426950408889634

    def norm(v, e):
        up = 2.0 * jnp.floor(0.5 * log2(largest(v)) + 0.5)
        return v * jnp.exp2(-up), e + up

    def add(terms):
        top = terms[0][1]
        for _, e in terms[1:]:
            top = jnp.maximum(top, e)
        value = None
        for m, e in terms:
            part = m * jnp.exp2(e - top)
            value = part if value is None else value + part
        return value, top

    def post(m, value, e):
        outbox[m, :B, :] = value
        outbox[m, B:, :] = jnp.broadcast_to(0.5 * e, (AUX, B)).astype(BF16)
        send(m)

    def take(m, far):
        i = SENDS.index((m, far))
        box_copy(i).wait_recv()
        there = jnp.logical_and(q - far >= 0, q - far < NQ)
        value = jnp.where(there, inbox[i, :B, :].astype(F32), 0.0)
        return value, inbox[i, B:, :].astype(F32)[:1, :1]

    def take_scaled(m, far):
        value, e = take(m, far)
        return value, 2.0 * e

    def size(m, e):
        return log2(total(m * m)) + 2.0 * e

    x = outbox[0, :B, :]
    xx = twice(x)
    start_l, rank_l = take(0, 1)
    start_r, rank_r = take(0, -1)
    hop = 0.5 * (start_l + start_r)
    acc = None
    for group in GROUPS:
        for p in group:
            for w in ORDER[2 * p:2 * p + 2]:
                pltpu.make_async_copy(recv.at[w], recv.at[w], recv_sem.at[w]).wait()
        part = pairs(xx, group)
        acc = part if acc is None else acc + part
    m1, l1 = norm(mask * (acc + hop), jnp.zeros((1, 1), F32))
    x1 = m1.astype(BF16)
    post(1, x1, l1)
    mp, lp = norm(apply(x1), l1)
    post(2, mp.astype(BF16), lp)
    sizes = [size(m1, l1)]
    half = 0.5 * mask
    half_l = jnp.where(larger < rank_l, 0.5, 0.0).astype(F32)
    half_r = jnp.where(larger < rank_r, 0.5, 0.0).astype(F32)
    m1_l, l1_l = take_scaled(1, 1)
    m1_r, l1_r = take_scaled(1, -1)
    m2, l2 = norm(*add([(mp, lp), (half * m1_l, l1_l), (half * m1_r, l1_r)]))
    r, lr = norm(apply(m2.astype(BF16)), l2)
    sizes.append(size(m2, l2))
    m1_ll, l1_ll = take_scaled(1, 2)
    m1_rr, l1_rr = take_scaled(1, -2)
    mp_l, lp_l = take_scaled(2, 1)
    mp_r, lp_r = take_scaled(2, -1)
    m2_l, l2_l = add([(mp_l, lp_l), (half_l * m1, l1), (half_l * m1_ll, l1_ll)])
    m2_r, l2_r = add([(mp_r, lp_r), (half_r * m1, l1), (half_r * m1_rr, l1_rr)])
    m2_l = jnp.where(q > 0, m2_l, 0.0)
    m2_r = jnp.where(q < NQ - 1, m2_r, 0.0)
    m3, l3 = norm(*add([(r, lr), (half * m2_l, l2_l), (half * m2_r, l2_r)]))
    x3 = m3.astype(BF16)
    post(3, x3, l3)
    v, lv = norm(apply(x3), l3)
    sizes.append(size(m3, l3))
    for t in range(B // ROWS):
        rows = recv[:, t * ROWS:(t + 1) * ROWS, :].reshape(KR, B)
        env_out[:, t * ROWS:(t + 1) * ROWS, :] = dot(big, rows).astype(BF16).reshape(WM, ROWS, B)
    m3_l, l3_l = take_scaled(3, 1)
    m3_r, l3_r = take_scaled(3, -1)
    m4, l4 = norm(*add([(v, lv), (half * m3_l, l3_l), (half * m3_r, l3_r)]))
    sizes.append(size(m4, l4))

    lane = lax.broadcasted_iota(jnp.int32, (1, B), 1)
    line = jnp.full((1, B), -1e30, F32)
    for k in range(ITERS):
        line = jnp.where(lane == k, sizes[k] + ((ITERS - 1 - k) * LOG_EPS - LOG_N), line)
    psend[...] = line
    pall[q] = line

    def sum_copy(i):
        return pltpu.make_async_remote_copy(
            src_ref=psend, dst_ref=pall.at[q], send_sem=psem, recv_sem=precv,
            device_id=(g, lax.rem(q + i, NQ)), device_id_type=MESH,
        )

    def start_sum(i, carry):
        sum_copy(i).start()
        return carry

    lax.fori_loop(1, NQ, start_sum, 0)

    def drain(s, carry):
        for j in range(SLOTS):
            def body(j=j):
                each_halo(s, j, lambda c: c.wait_send())
                each_halo2(s, j, lambda c: c.wait_send())

                @pl.when(g != s + 1)
                def _():
                    deliver(s + 1, j).wait_send()

            each_slot(j, body)

        @pl.when(forwards(s))
        def _():
            forward(s).wait_send()

        each_far_trans(s, lambda c: c.wait_send())
        return carry

    lax.fori_loop(0, STEPS, drain, 0)
    each_trans(lambda c: c.wait_send())

    @pl.when(g < STEPS)
    def _():
        for i in range(1, NS):
            mix_copy(i).wait_send()

    for i in range(len(SENDS)):
        box_copy(i).wait_send()
    others = pall.at[pl.ds(0, NQ - 1)]
    pltpu.make_async_copy(others, others, psem).wait()
    pltpu.make_async_copy(others, others, precv).wait()
    logs = pall[...].reshape(NQ, B)
    top = jnp.max(jnp.max(logs, axis=0, keepdims=True), axis=1, keepdims=True)
    top = jnp.maximum(top, ITERS * LOG_EPS)
    square = total(jnp.exp2(logs - top)) + jnp.exp2(ITERS * LOG_EPS - top)
    state[...] = m4 * (jnp.exp2(l4 - 0.5 * top) * lax.rsqrt(square))


def per_device(env_left, transfer, mpo_mix, right_env, start_state, block_rank):
    dma = pltpu.SemaphoreType.DMA
    vmem = pl.BlockSpec(memory_space=pltpu.VMEM)
    hbm = pl.BlockSpec(memory_space=pltpu.HBM)
    state, env = pl.pallas_call(
        kernel,
        out_shape=(
            jax.ShapeDtypeStruct((B, B), F32),
            jax.ShapeDtypeStruct((WM, B, B), BF16),
        ),
        in_specs=[hbm, hbm, hbm, hbm, hbm, pl.BlockSpec(memory_space=pltpu.SMEM)],
        out_specs=(vmem, vmem),
        scratch_shapes=[
            pltpu.VMEM((NS, SLOTS, B, B), BF16),
            pltpu.VMEM((STEPS, 2, SLOTS, B, B), BF16),
            pltpu.VMEM((3, SLOTS, B, B), BF16),
            pltpu.VMEM((3, 3 * B, B), BF16),
            pltpu.VMEM((3, B, B), BF16),
            pltpu.VMEM((WM, B, B), BF16),
            pltpu.VMEM((WM, B, B), BF16),
            pltpu.VMEM((PAIRS, 2 * B, B), BF16),
            pltpu.VMEM((NS, 3 * B, B), BF16),
            pltpu.VMEM((3, B, B), BF16),
            pltpu.VMEM((NS, 32, B), F32),
            pltpu.VMEM((32, B), F32),
            pltpu.VMEM((WM, 1, WM), F32),
            pltpu.VMEM((32, B), F32),
            pltpu.VMEM((B, B), F32),
            pltpu.VMEM((4, MSG, B), BF16),
            pltpu.VMEM((len(SENDS), MSG, B), BF16),
            pltpu.VMEM((1, B), F32),
            pltpu.VMEM((NQ, 1, B), F32),
            dma((SLOTS,)),
            dma((4,)),
            dma((WM,)),
            dma((NS, SLOTS)),
            dma((STEPS, 2, SLOTS)),
            dma((STEPS, 2, SLOTS)),
            dma((3, SLOTS)),
            dma((3, SLOTS)),
            dma((3,)),
            dma((3, 2)),
            dma((NS,)),
            dma((NS,)),
            dma((NS,)),
            dma((NS,)),
            dma((NS,)),
            dma((len(SENDS),)),
            dma((len(SENDS),)),
            dma,
            dma,
            pltpu.SemaphoreType.REGULAR((3,)),
        ],
        compiler_params=pltpu.CompilerParams(
            collective_id=0, has_side_effects=True, vmem_limit_bytes=40 * 1024 * 1024
        ),
    )(
        *(
            pltpu.with_memory_space_constraint(value, pltpu.HBM)
            for value in (
                env_left.reshape(WM, B, B),
                transfer.reshape(3 * B, B),
                jnp.transpose(mpo_mix, (1, 0, 2)),
                right_env.reshape(WM, B, B),
                start_state.reshape(B, B),
            )
        ),
        block_rank,
    )
    return state.reshape(1, 1, B, B), env.reshape(1, WM, 1, B, B)


def solution(mesh):
    in_specs = (
        P(None, "blk", None, None),
        P("sec", "blk", None, None, None),
        P("sec", None, None),
        P("sec", None, "blk", None, None),
        P("sec", "blk", None, None),
        P("blk"),
    )
    out_specs = (P("sec", "blk", None, None), P("sec", None, "blk", None, None))
    return jax.shard_map(
        per_device, mesh=mesh, in_specs=in_specs, out_specs=out_specs, check_vma=False
    )
```

```python
import jax
import jax.numpy as jnp
from jax import lax
from jax.experimental import pallas as pl
from jax.experimental.pallas import tpu as pltpu
from jax.sharding import PartitionSpec as P

ITERS = 4
B = 128
WM = 26
NS = 8
NQ = 32
NX = 4
NEAR = (1, NQ - 1, 2, NQ - 2)
SLOTS = 4
STEPS = NS - 1
PAIRS = WM // 2
ROWS = 16
KR = WM * ROWS
FIRSTS = (0, 4, 7, 11, 14, 17, 20, 23)
ORDER = [f + j for j in range(3) for f in FIRSTS] + [3, 10]
GROUPS = (range(0, 4), range(4, 8), range(8, 13))
AUX = 16
MSG = B + AUX
SENDS = ((0, 1), (0, -1), (1, 1), (1, -1), (1, 2), (1, -2), (2, 1), (2, -1), (3, 1), (3, -1))
LOG_EPS = -19.931568569324174
LOG_N = 19.0
MESH = pl.DeviceIdType.MESH
F32 = jnp.float32
BF16 = jnp.bfloat16


def dot(a, b):
    return jnp.dot(a, b, preferred_element_type=F32)


def kernel(
    env_hbm, trans_hbm, mix_hbm, renv_hbm, start_hbm, rank, state, env_out,
    raw, halo, halo2, fart, ft, recv, renv, renvp, tall, tt, mixall, amat, mix_in, own_mix,
    start, outbox, inbox, psend, pall,
    load_sem, in_sem, recv_sem, deliver_sem,
    hrecv, hsend, h2recv, h2send, ftrecv, ftsend, trecv, tsend, fsend, mrecv, msend,
    xrecv, xsem, precv, psem, known,
):
    g = lax.axis_index("sec")
    q = lax.axis_index("blk")
    y = g // 2
    core = lax.rem(g, 2)
    right = lax.rem(q + 1, NQ)
    left = lax.rem(q + NQ - 1, NQ)
    first = 3 * g + jnp.where(g >= 1, 1, 0) + jnp.where(g >= 3, 1, 0)
    four = jnp.logical_or(g == 0, g == 2)
    x_at = lax.rem(q, NX)
    far = jnp.logical_or(x_at == 0, x_at == NX - 1)
    side = jnp.where(x_at == 0, 0, 1)
    beyond = jnp.where(x_at == 0, left, right)
    two_off = lax.rem(jnp.where(x_at == 2, q + 2, q + (NQ - 2)), NQ)

    barrier = pltpu.get_barrier_semaphore()

    def greet_sec(i, carry):
        pl.semaphore_signal(barrier, inc=1, device_id=(lax.rem(g + i, NS), q), device_id_type=MESH)
        return carry

    lax.fori_loop(1, NS, greet_sec, 0)
    for i in NEAR:
        pl.semaphore_signal(barrier, inc=1, device_id=(g, lax.rem(q + i, NQ)), device_id_type=MESH)

    @pl.when(jnp.logical_and(far, core == 0))
    def _():
        pl.semaphore_signal(barrier, inc=1, device_id=(g + 1, beyond), device_id_type=MESH)


    loads = [
        pltpu.make_async_copy(trans_hbm, tall.at[g], in_sem.at[0]),
        pltpu.make_async_copy(mix_hbm, mix_in, in_sem.at[1]),
        pltpu.make_async_copy(start_hbm, start, in_sem.at[2]),
        pltpu.make_async_copy(renv_hbm, renv, in_sem.at[3]),
    ]

    def each_slot(j, body):
        if j < SLOTS - 1:
            body()
        else:
            pl.when(four)(body)

    def load(j):
        return pltpu.make_async_copy(env_hbm.at[first + j], raw.at[0, j], load_sem.at[j])

    loads[0].start()
    for j in range(SLOTS):
        each_slot(j, lambda j=j: load(j).start())
    for c in loads[1:]:
        c.start()

    @pl.when(g == 0)
    def _():
        def body(w, carry):
            pltpu.make_async_copy(env_hbm.at[w], recv.at[w], recv_sem.at[w]).start()
            return carry

        lax.fori_loop(0, WM, body, 0)

    own_mix[...] = jnp.zeros_like(own_mix)
    loads[1].wait()
    own_mix[:WM, :WM] = mix_in[...].reshape(WM, WM)
    mixall[g] = own_mix[...]
    row = lax.broadcasted_iota(jnp.int32, (32, B), 0)
    col = lax.broadcasted_iota(jnp.int32, (32, B), 1)
    amat[...] = jnp.where(row == col, 1.0, 0.0).astype(F32)
    keep0 = lax.broadcasted_iota(jnp.int32, (B, B), 0)
    keep1 = lax.broadcasted_iota(jnp.int32, (B, B), 1)
    larger = jnp.maximum(keep0, keep1).astype(F32)
    my_rank = rank[0].astype(F32)
    mask = jnp.where(larger < my_rank, 1.0, 0.0).astype(F32)
    loads[2].wait()
    outbox[0, :B, :] = (start[...] * mask).astype(BF16)
    outbox[0, B:, :] = jnp.full((AUX, B), my_rank, F32).astype(BF16)
    loads[0].wait()
    for j in range(SLOTS):
        each_slot(j, lambda j=j: load(j).wait())

    pl.semaphore_wait(barrier, NS - 1 + len(NEAR) + jnp.where(jnp.logical_and(far, core == 1), 1, 0))

    def crossed(s):
        return jnp.logical_or(s == 0, lax.rem(s, 2) == 1)

    def halo_copy(s, j, to):
        return pltpu.make_async_remote_copy(
            src_ref=raw.at[s, j], dst_ref=halo.at[s, 1 - to, j],
            send_sem=hsend.at[s, to, j], recv_sem=hrecv.at[s, 1 - to, j],
            device_id=(g, right if to else left), device_id_type=MESH,
        )

    def inside(to):
        return x_at != (NX - 1 if to else 0)

    def each_halo(s, j, act):
        for to in range(2):
            pl.when(jnp.logical_or(inside(to), crossed(s)))(lambda to=to: act(halo_copy(s, j, to)))

    def wait_halo(s, j):
        for at in range(2):
            @pl.when(jnp.logical_or(inside(at), crossed(s)))
            def _():
                halo_copy(s, j, 1 - at).wait_recv()

    def halo2_copy(s, j):
        return pltpu.make_async_remote_copy(
            src_ref=raw.at[s, j], dst_ref=halo2.at[s // 2, j],
            send_sem=h2send.at[s // 2, j], recv_sem=h2recv.at[s // 2, j],
            device_id=(g, two_off), device_id_type=MESH,
        )

    def each_halo2(s, j, act):
        pl.when(jnp.logical_and(jnp.logical_not(far), lax.rem(s, 2) == 1))(lambda: act(halo2_copy(s, j)))

    def start_halo(s, j):
        each_halo(s, j, lambda c: c.start())
        each_halo2(s, j, lambda c: c.start())

    def far_trans(s, i):
        return pltpu.make_async_remote_copy(
            src_ref=tall.at[s], dst_ref=fart.at[s // 2],
            send_sem=ftsend.at[s // 2, i], recv_sem=ftrecv.at[s // 2],
            device_id=(g - i, beyond), device_id_type=MESH,
        )

    def each_far_trans(s, act):
        @pl.when(jnp.logical_and(jnp.logical_and(far, core == 1), jnp.logical_and(lax.rem(s, 2) == 1, s < STEPS)))
        def _():
            for i in range(2):
                act(far_trans(s, i))

    def trans_copy(src, s, sem, other):
        return pltpu.make_async_remote_copy(
            src_ref=src, dst_ref=tall.at[s], send_sem=sem, recv_sem=trecv.at[s],
            device_id=(other, q), device_id_type=MESH,
        )

    def mix_copy(i):
        return pltpu.make_async_remote_copy(
            src_ref=own_mix, dst_ref=mixall.at[g], send_sem=msend.at[i], recv_sem=mrecv.at[g],
            device_id=(lax.rem(g + i, NS), q), device_id_type=MESH,
        )

    def each_trans(act):
        @pl.when(g == 0)
        def _():
            for i in range(1, NS):
                act(trans_copy(tall.at[g], 0, tsend.at[i], i))

        @pl.when(jnp.logical_and(g > 0, g < STEPS))
        def _():
            act(trans_copy(tall.at[g], g, tsend.at[0], g + 1 - 2 * core))
            for i in range(1, 4):
                act(trans_copy(tall.at[g], g, tsend.at[i], lax.rem(g + 2 * i, NS)))

    for j in range(SLOTS):
        each_slot(j, lambda j=j: start_halo(0, j))
    each_trans(lambda c: c.start())

    @pl.when(g < STEPS)
    def _():
        for i in range(1, NS):
            mix_copy(i).start()

    def box_copy(i):
        m, far = SENDS[i]
        return pltpu.make_async_remote_copy(
            src_ref=outbox.at[m], dst_ref=inbox.at[i], send_sem=xsem.at[i], recv_sem=xrecv.at[i],
            device_id=(g, lax.rem(q + (NQ + far), NQ)), device_id_type=MESH,
        )

    def send(m):
        for i in range(len(SENDS)):
            if SENDS[i][0] == m:
                box_copy(i).start()

    send(0)

    def deliver(s, j):
        return pltpu.make_async_remote_copy(
            src_ref=raw.at[s, j], dst_ref=recv.at[first + j],
            send_sem=deliver_sem.at[s, j], recv_sem=recv_sem.at[first + j],
            device_id=(s, q), device_id_type=MESH,
        )

    def deliver_local(s, j):
        return pltpu.make_async_copy(raw.at[s, j], recv.at[first + j], recv_sem.at[first + j])

    def forwards(s):
        return jnp.logical_and(
            jnp.logical_and(core == lax.rem(s, 2), y != s // 2), jnp.logical_and(s >= 1, s < STEPS)
        )

    def forward(s):
        return trans_copy(tall.at[s], s, fsend.at[s], g + 1 - 2 * core)

    def wait_trans(s):
        pltpu.make_async_copy(tall.at[s], tall.at[s], trecv.at[s]).wait()

    def pass_on(s):
        @pl.when(forwards(s))
        def _():
            wait_trans(s)
            forward(s).start()

        each_far_trans(s, lambda c: c.start())

    pass_on(1)

    def tell(i):
        far_off = 2 << i
        for other in (q + far_off, q + (NQ - far_off)):
            pl.semaphore_signal(known.at[i], inc=1, device_id=(g, lax.rem(other, NQ)), device_id_type=MESH)

    def heard(i):
        pl.semaphore_wait(known.at[i], 2)

    tell(0)

    def step(s, carry):
        for i in range(3):
            @pl.when(s == i + 1)
            def _():
                heard(i)
                if i < 2:
                    tell(i + 1)

        @pl.when(jnp.logical_and(g != s, jnp.logical_not(forwards(s))))
        def _():
            wait_trans(s)

        redo = jnp.logical_and(far, lax.rem(s, 2) == 1)

        for d in range(3):
            t = tall[s, d * B:(d + 1) * B, :].T
            if d == 0:
                t = jnp.where(q > 0, t, jnp.zeros_like(t))
            if d == 2:
                t = jnp.where(q < NQ - 1, t, jnp.zeros_like(t))
            tt[d] = t

        def carry_on(parts, turned, tensor):
            parts = [dot(turned[d], parts[d]).astype(BF16) for d in range(3)]
            return dot(jnp.concatenate(parts, axis=1), tensor).astype(BF16)

        for j in range(SLOTS):
            def body(j=j):
                wait_halo(s, j)
                raw[s + 1, j] = carry_on([halo[s, 0, j], raw[s, j], halo[s, 1, j]], tt, tall[s])

                @pl.when(s < STEPS - 1)
                def _():
                    start_halo(s + 1, j)

                @pl.when(g != s + 1)
                def _():
                    deliver(s + 1, j).start()

                @pl.when(g == s + 1)
                def _():
                    deliver_local(s + 1, j).start()

            each_slot(j, body)

        @pl.when(s == 0)
        def _():
            for i in range(2, STEPS):
                pass_on(i)

        @pl.when(redo)
        def _():
            pltpu.make_async_copy(fart.at[s // 2], fart.at[s // 2], ftrecv.at[s // 2]).wait()
            for d in range(3):
                ft[d] = fart[s // 2, d * B:(d + 1) * B, :].T
            for j in range(SLOTS):
                def again(j=j):
                    halo2_copy(s, j).wait_recv()
                    mine, other = raw[s, j], halo2[s // 2, j]
                    low = jnp.where(x_at == 0, other, mine)
                    high = jnp.where(x_at == 0, mine, other)
                    halo[s + 1, side, j] = carry_on([low, halo[s, side, j], high], ft, fart[s // 2])

                each_slot(j, again)

        @pl.when(g != s)
        def _():
            pltpu.make_async_copy(mixall.at[s], mixall.at[s], mrecv.at[s]).wait()

        @pl.when(s < g)
        def _():
            amat[...] = jnp.dot(mixall[s][:, :32], amat[...], precision=lax.Precision.HIGHEST, preferred_element_type=F32)

        return carry

    lax.fori_loop(0, STEPS, step, 0)

    a = amat[...][:, :32].astype(BF16)
    wide = lax.broadcasted_iota(jnp.int32, (KR, 32), 0) // ROWS
    spread = jnp.where(wide == lax.broadcasted_iota(jnp.int32, (KR, 32), 1), 1.0, 0.0).astype(BF16)
    r0 = lax.rem(lax.broadcasted_iota(jnp.int32, (KR, KR), 0), ROWS)
    r1 = lax.rem(lax.broadcasted_iota(jnp.int32, (KR, KR), 1), ROWS)

    def widen(half):
        full = lax.dot_general(half.astype(BF16), spread, (((1,), (1,)), ((), ())), preferred_element_type=F32)
        return jnp.where(r0 == r1, full, 0.0).astype(BF16)

    turned = widen(lax.dot_general(spread, a, (((1,), (1,)), ((), ())), preferred_element_type=F32))
    loads[3].wait()
    for t in range(B // ROWS):
        rows = renv[:, t * ROWS:(t + 1) * ROWS, :].reshape(KR, B)
        mixed = dot(turned, rows).astype(BF16).reshape(WM, ROWS, B)
        for i, w in enumerate(ORDER):
            at = (i % 2) * B + t * ROWS
            renvp[i // 2, at:at + ROWS, :] = mixed[w]
    big = widen(dot(spread, a))

    def pairs(xx, group):
        acc = None
        for p in group:
            pair = jnp.concatenate([recv[ORDER[2 * p]], recv[ORDER[2 * p + 1]]], axis=1)
            term = dot(dot(pair, xx).astype(BF16), renvp[p])
            acc = term if acc is None else acc + term
        return acc

    def twice(x):
        zero = jnp.zeros_like(x)
        return jnp.concatenate([jnp.concatenate([x, zero], axis=1), jnp.concatenate([zero, x], axis=1)], axis=0)

    def apply(x):
        return pairs(twice(x), range(PAIRS)) * mask

    def largest(v):
        return jnp.max(jnp.max(jnp.abs(v), axis=0, keepdims=True), axis=1, keepdims=True)

    def total(v):
        return jnp.sum(jnp.sum(v, axis=0, keepdims=True), axis=1, keepdims=True)

    def log2(v):
        return jnp.log(jnp.maximum(v, 1e-30)) * 1.4426950408889634

    def norm(v, e):
        up = 2.0 * jnp.floor(0.5 * log2(largest(v)) + 0.5)
        return v * jnp.exp2(-up), e + up

    def add(terms):
        top = terms[0][1]
        for _, e in terms[1:]:
            top = jnp.maximum(top, e)
        value = None
        for m, e in terms:
            part = m * jnp.exp2(e - top)
            value = part if value is None else value + part
        return value, top

    def post(m, value, e):
        outbox[m, :B, :] = value
        outbox[m, B:, :] = jnp.broadcast_to(0.5 * e, (AUX, B)).astype(BF16)
        send(m)

    def take(m, far):
        i = SENDS.index((m, far))
        box_copy(i).wait_recv()
        there = jnp.logical_and(q - far >= 0, q - far < NQ)
        value = jnp.where(there, inbox[i, :B, :].astype(F32), 0.0)
        return value, inbox[i, B:, :].astype(F32)[:1, :1]

    def take_scaled(m, far):
        value, e = take(m, far)
        return value, 2.0 * e

    def size(m, e):
        return log2(total(m * m)) + 2.0 * e

    x = outbox[0, :B, :]
    xx = twice(x)
    start_l, rank_l = take(0, 1)
    start_r, rank_r = take(0, -1)
    hop = 0.5 * (start_l + start_r)
    acc = None
    for group in GROUPS:
        for p in group:
            for w in ORDER[2 * p:2 * p + 2]:
                pltpu.make_async_copy(recv.at[w], recv.at[w], recv_sem.at[w]).wait()
        part = pairs(xx, group)
        acc = part if acc is None else acc + part
    m1, l1 = norm(mask * (acc + hop), jnp.zeros((1, 1), F32))
    x1 = m1.astype(BF16)
    post(1, x1, l1)
    mp, lp = norm(apply(x1), l1)
    post(2, mp.astype(BF16), lp)
    sizes = [size(m1, l1)]
    half = 0.5 * mask
    half_l = jnp.where(larger < rank_l, 0.5, 0.0).astype(F32)
    half_r = jnp.where(larger < rank_r, 0.5, 0.0).astype(F32)
    m1_l, l1_l = take_scaled(1, 1)
    m1_r, l1_r = take_scaled(1, -1)
    m2, l2 = norm(*add([(mp, lp), (half * m1_l, l1_l), (half * m1_r, l1_r)]))
    r, lr = norm(apply(m2.astype(BF16)), l2)
    sizes.append(size(m2, l2))
    m1_ll, l1_ll = take_scaled(1, 2)
    m1_rr, l1_rr = take_scaled(1, -2)
    mp_l, lp_l = take_scaled(2, 1)
    mp_r, lp_r = take_scaled(2, -1)
    m2_l, l2_l = add([(mp_l, lp_l), (half_l * m1, l1), (half_l * m1_ll, l1_ll)])
    m2_r, l2_r = add([(mp_r, lp_r), (half_r * m1, l1), (half_r * m1_rr, l1_rr)])
    m2_l = jnp.where(q > 0, m2_l, 0.0)
    m2_r = jnp.where(q < NQ - 1, m2_r, 0.0)
    m3, l3 = norm(*add([(r, lr), (half * m2_l, l2_l), (half * m2_r, l2_r)]))
    x3 = m3.astype(BF16)
    post(3, x3, l3)
    v, lv = norm(apply(x3), l3)
    sizes.append(size(m3, l3))
    for t in range(B // ROWS):
        rows = recv[:, t * ROWS:(t + 1) * ROWS, :].reshape(KR, B)
        env_out[:, t * ROWS:(t + 1) * ROWS, :] = dot(big, rows).astype(BF16).reshape(WM, ROWS, B)
    m3_l, l3_l = take_scaled(3, 1)
    m3_r, l3_r = take_scaled(3, -1)
    m4, l4 = norm(*add([(v, lv), (half * m3_l, l3_l), (half * m3_r, l3_r)]))
    sizes.append(size(m4, l4))

    lane = lax.broadcasted_iota(jnp.int32, (1, B), 1)
    line = jnp.full((1, B), -1e30, F32)
    for k in range(ITERS):
        line = jnp.where(lane == k, sizes[k] + ((ITERS - 1 - k) * LOG_EPS - LOG_N), line)
    psend[...] = line
    pall[q] = line

    def sum_copy(i):
        return pltpu.make_async_remote_copy(
            src_ref=psend, dst_ref=pall.at[q], send_sem=psem, recv_sem=precv,
            device_id=(g, lax.rem(q + i, NQ)), device_id_type=MESH,
        )

    def start_sum(i, carry):
        sum_copy(i).start()
        return carry

    lax.fori_loop(1, NQ, start_sum, 0)

    def drain(s, carry):
        for j in range(SLOTS):
            def body(j=j):
                each_halo(s, j, lambda c: c.wait_send())
                each_halo2(s, j, lambda c: c.wait_send())

                @pl.when(g != s + 1)
                def _():
                    deliver(s + 1, j).wait_send()

            each_slot(j, body)

        @pl.when(forwards(s))
        def _():
            forward(s).wait_send()

        each_far_trans(s, lambda c: c.wait_send())
        return carry

    lax.fori_loop(0, STEPS, drain, 0)
    each_trans(lambda c: c.wait_send())

    @pl.when(g < STEPS)
    def _():
        for i in range(1, NS):
            mix_copy(i).wait_send()

    for i in range(len(SENDS)):
        box_copy(i).wait_send()
    others = pall.at[pl.ds(0, NQ - 1)]
    pltpu.make_async_copy(others, others, psem).wait()
    pltpu.make_async_copy(others, others, precv).wait()
    logs = pall[...].reshape(NQ, B)
    top = jnp.max(jnp.max(logs, axis=0, keepdims=True), axis=1, keepdims=True)
    top = jnp.maximum(top, ITERS * LOG_EPS)
    square = total(jnp.exp2(logs - top)) + jnp.exp2(ITERS * LOG_EPS - top)
    state[...] = m4 * (jnp.exp2(l4 - 0.5 * top) * lax.rsqrt(square))


def per_device(env_left, transfer, mpo_mix, right_env, start_state, block_rank):
    dma = pltpu.SemaphoreType.DMA
    vmem = pl.BlockSpec(memory_space=pltpu.VMEM)
    hbm = pl.BlockSpec(memory_space=pltpu.HBM)
    state, env = pl.pallas_call(
        kernel,
        out_shape=(
            jax.ShapeDtypeStruct((B, B), F32),
            jax.ShapeDtypeStruct((WM, B, B), BF16),
        ),
        in_specs=[hbm, hbm, hbm, hbm, hbm, pl.BlockSpec(memory_space=pltpu.SMEM)],
        out_specs=(vmem, vmem),
        scratch_shapes=[
            pltpu.VMEM((NS, SLOTS, B, B), BF16),
            pltpu.VMEM((STEPS, 2, SLOTS, B, B), BF16),
            pltpu.VMEM((3, SLOTS, B, B), BF16),
            pltpu.VMEM((3, 3 * B, B), BF16),
            pltpu.VMEM((3, B, B), BF16),
            pltpu.VMEM((WM, B, B), BF16),
            pltpu.VMEM((WM, B, B), BF16),
            pltpu.VMEM((PAIRS, 2 * B, B), BF16),
            pltpu.VMEM((NS, 3 * B, B), BF16),
            pltpu.VMEM((3, B, B), BF16),
            pltpu.VMEM((NS, 32, B), F32),
            pltpu.VMEM((32, B), F32),
            pltpu.VMEM((WM, 1, WM), F32),
            pltpu.VMEM((32, B), F32),
            pltpu.VMEM((B, B), F32),
            pltpu.VMEM((4, MSG, B), BF16),
            pltpu.VMEM((len(SENDS), MSG, B), BF16),
            pltpu.VMEM((1, B), F32),
            pltpu.VMEM((NQ, 1, B), F32),
            dma((SLOTS,)),
            dma((4,)),
            dma((WM,)),
            dma((NS, SLOTS)),
            dma((STEPS, 2, SLOTS)),
            dma((STEPS, 2, SLOTS)),
            dma((3, SLOTS)),
            dma((3, SLOTS)),
            dma((3,)),
            dma((3, 2)),
            dma((NS,)),
            dma((NS,)),
            dma((NS,)),
            dma((NS,)),
            dma((NS,)),
            dma((len(SENDS),)),
            dma((len(SENDS),)),
            dma,
            dma,
            pltpu.SemaphoreType.REGULAR((3,)),
        ],
        compiler_params=pltpu.CompilerParams(
            collective_id=0, has_side_effects=True, vmem_limit_bytes=40 * 1024 * 1024
        ),
    )(
        *(
            pltpu.with_memory_space_constraint(value, pltpu.HBM)
            for value in (
                env_left.reshape(WM, B, B),
                transfer.reshape(3 * B, B),
                jnp.transpose(mpo_mix, (1, 0, 2)),
                right_env.reshape(WM, B, B),
                start_state.reshape(B, B),
            )
        ),
        block_rank,
    )
    return state.reshape(1, 1, B, B), env.reshape(1, WM, 1, B, B)


def solution(mesh):
    in_specs = (
        P(None, "blk", None, None),
        P("sec", "blk", None, None, None),
        P("sec", None, None),
        P("sec", None, "blk", None, None),
        P("sec", "blk", None, None),
        P("blk"),
    )
    out_specs = (P("sec", "blk", None, None), P("sec", None, "blk", None, None))
    return jax.shard_map(
        per_device, mesh=mesh, in_specs=in_specs, out_specs=out_specs, check_vma=False
    )
```

```python
import jax
import jax.numpy as jnp
from jax import lax
from jax.experimental import pallas as pl
from jax.experimental.pallas import tpu as pltpu
from jax.sharding import PartitionSpec as P

ITERS = 4
B = 128
WM = 26
NS = 8
NQ = 32
NX = 4
NEAR = (1, -1, 2, -2)
SLOTS = 4
STEPS = NS - 1
PAIRS = WM // 2
ROWS = 16
KR = WM * ROWS
FIRSTS = (0, 4, 7, 11, 14, 17, 20, 23)
ORDER = [f + j for j in range(3) for f in FIRSTS] + [3, 10]
GROUPS = (range(0, 4), range(4, 8), range(8, 13))
AUX = 16
MSG = B + AUX
SENDS = ((0, 1), (0, -1), (1, 1), (1, -1), (1, 2), (1, -2), (2, 1), (2, -1), (3, 1), (3, -1))
LOG_EPS = -19.931568569324174
LOG_N = 19.0
MESH = pl.DeviceIdType.MESH
F32 = jnp.float32
BF16 = jnp.bfloat16


def dot(a, b):
    return jnp.dot(a, b, preferred_element_type=F32)


def kernel(
    env_hbm, trans_hbm, mix_hbm, renv_hbm, start_hbm, rank, state, env_out,
    raw, halo, halo2, fart, ft, recv, renv, renvp, tall, tt, mixall, amat, mix_in, own_mix,
    start, outbox, inbox, psend, pall,
    load_sem, in_sem, recv_sem, deliver_sem,
    hrecv, hsend, h2recv, h2send, ftrecv, ftsend, trecv, tsend, fsend, mrecv, msend,
    xrecv, xsem, precv, psem, known,
):
    g = lax.axis_index("sec")
    q = lax.axis_index("blk")
    y = g // 2
    core = lax.rem(g, 2)
    right = lax.rem(q + 1, NQ)
    left = lax.rem(q + NQ - 1, NQ)
    first = 3 * g + jnp.where(g >= 1, 1, 0) + jnp.where(g >= 3, 1, 0)
    four = jnp.logical_or(g == 0, g == 2)
    x_at = lax.rem(q, NX)
    low_end, high_end = q == 0, q == NQ - 1
    at_low = jnp.logical_and(x_at == 0, jnp.logical_not(low_end))
    at_high = jnp.logical_and(x_at == NX - 1, jnp.logical_not(high_end))
    far = jnp.logical_or(at_low, at_high)
    gives = jnp.logical_or(jnp.logical_and(x_at == 1, q > NX), jnp.logical_and(x_at == 2, q < NQ - NX))

    def exists(other):
        return jnp.logical_and(other >= 0, other < NQ)

    side = jnp.where(x_at == 0, 0, 1)
    beyond = jnp.where(x_at == 0, left, right)
    two_off = lax.rem(jnp.where(x_at == 2, q + 2, q + (NQ - 2)), NQ)

    barrier = pltpu.get_barrier_semaphore()

    def greet_sec(i, carry):
        pl.semaphore_signal(barrier, inc=1, device_id=(lax.rem(g + i, NS), q), device_id_type=MESH)
        return carry

    lax.fori_loop(1, NS, greet_sec, 0)
    greeted = NS - 1 + jnp.where(jnp.logical_and(far, core == 1), 1, 0)
    for i in NEAR:
        @pl.when(exists(q + i))
        def _():
            pl.semaphore_signal(barrier, inc=1, device_id=(g, q + i), device_id_type=MESH)

        greeted += jnp.where(exists(q + i), 1, 0)

    @pl.when(jnp.logical_and(far, core == 0))
    def _():
        pl.semaphore_signal(barrier, inc=1, device_id=(g + 1, beyond), device_id_type=MESH)


    loads = [
        pltpu.make_async_copy(trans_hbm, tall.at[g], in_sem.at[0]),
        pltpu.make_async_copy(mix_hbm, mix_in, in_sem.at[1]),
        pltpu.make_async_copy(start_hbm, start, in_sem.at[2]),
        pltpu.make_async_copy(renv_hbm, renv, in_sem.at[3]),
    ]

    def each_slot(j, body):
        if j < SLOTS - 1:
            body()
        else:
            pl.when(four)(body)

    def load(j):
        return pltpu.make_async_copy(env_hbm.at[first + j], raw.at[0, j], load_sem.at[j])

    loads[0].start()
    for j in range(SLOTS):
        each_slot(j, lambda j=j: load(j).start())
    for c in loads[1:]:
        c.start()

    @pl.when(g == 0)
    def _():
        def body(w, carry):
            pltpu.make_async_copy(env_hbm.at[w], recv.at[w], recv_sem.at[w]).start()
            return carry

        lax.fori_loop(0, WM, body, 0)

    own_mix[...] = jnp.zeros_like(own_mix)
    for end, at in ((low_end, 0), (high_end, 1)):
        @pl.when(end)
        def _():
            def clear(s, carry):
                halo[s, at] = jnp.zeros((SLOTS, B, B), BF16)
                return carry

            lax.fori_loop(0, STEPS, clear, 0)

    loads[1].wait()
    own_mix[:WM, :WM] = mix_in[...].reshape(WM, WM)
    mixall[g] = own_mix[...]
    row = lax.broadcasted_iota(jnp.int32, (32, B), 0)
    col = lax.broadcasted_iota(jnp.int32, (32, B), 1)
    amat[...] = jnp.where(row == col, 1.0, 0.0).astype(F32)
    keep0 = lax.broadcasted_iota(jnp.int32, (B, B), 0)
    keep1 = lax.broadcasted_iota(jnp.int32, (B, B), 1)
    larger = jnp.maximum(keep0, keep1).astype(F32)
    my_rank = rank[0].astype(F32)
    mask = jnp.where(larger < my_rank, 1.0, 0.0).astype(F32)
    loads[2].wait()
    outbox[0, :B, :] = (start[...] * mask).astype(BF16)
    outbox[0, B:, :] = jnp.full((AUX, B), my_rank, F32).astype(BF16)
    loads[0].wait()
    for j in range(SLOTS):
        each_slot(j, lambda j=j: load(j).wait())

    pl.semaphore_wait(barrier, greeted)

    def crossed(s):
        return jnp.logical_or(s == 0, lax.rem(s, 2) == 1)

    def halo_copy(s, j, to):
        return pltpu.make_async_remote_copy(
            src_ref=raw.at[s, j], dst_ref=halo.at[s, 1 - to, j],
            send_sem=hsend.at[s, to, j], recv_sem=hrecv.at[s, 1 - to, j],
            device_id=(g, right if to else left), device_id_type=MESH,
        )

    def meets(to, s):
        end, at = (high_end, at_high) if to else (low_end, at_low)
        return jnp.logical_and(jnp.logical_not(end), jnp.logical_or(jnp.logical_not(at), crossed(s)))

    def each_halo(s, j, act):
        for to in range(2):
            pl.when(meets(to, s))(lambda to=to: act(halo_copy(s, j, to)))

    def wait_halo(s, j):
        for at in range(2):
            @pl.when(meets(at, s))
            def _():
                halo_copy(s, j, 1 - at).wait_recv()

    def halo2_copy(s, j):
        return pltpu.make_async_remote_copy(
            src_ref=raw.at[s, j], dst_ref=halo2.at[s // 2, j],
            send_sem=h2send.at[s // 2, j], recv_sem=h2recv.at[s // 2, j],
            device_id=(g, two_off), device_id_type=MESH,
        )

    def each_halo2(s, j, act):
        pl.when(jnp.logical_and(gives, lax.rem(s, 2) == 1))(lambda: act(halo2_copy(s, j)))

    def start_halo(s, j):
        each_halo(s, j, lambda c: c.start())
        each_halo2(s, j, lambda c: c.start())

    def far_trans(s, i):
        return pltpu.make_async_remote_copy(
            src_ref=tall.at[s], dst_ref=fart.at[s // 2],
            send_sem=ftsend.at[s // 2, i], recv_sem=ftrecv.at[s // 2],
            device_id=(g - i, beyond), device_id_type=MESH,
        )

    def each_far_trans(s, act):
        @pl.when(jnp.logical_and(jnp.logical_and(far, core == 1), jnp.logical_and(lax.rem(s, 2) == 1, s < STEPS)))
        def _():
            for i in range(2):
                act(far_trans(s, i))

    def trans_copy(src, s, sem, other):
        return pltpu.make_async_remote_copy(
            src_ref=src, dst_ref=tall.at[s], send_sem=sem, recv_sem=trecv.at[s],
            device_id=(other, q), device_id_type=MESH,
        )

    def mix_copy(i):
        return pltpu.make_async_remote_copy(
            src_ref=own_mix, dst_ref=mixall.at[g], send_sem=msend.at[i], recv_sem=mrecv.at[g],
            device_id=(lax.rem(g + i, NS), q), device_id_type=MESH,
        )

    def each_trans(act):
        @pl.when(g == 0)
        def _():
            for i in range(1, NS):
                act(trans_copy(tall.at[g], 0, tsend.at[i], i))

        @pl.when(jnp.logical_and(g > 0, g < STEPS))
        def _():
            act(trans_copy(tall.at[g], g, tsend.at[0], g + 1 - 2 * core))
            for i in range(1, 4):
                act(trans_copy(tall.at[g], g, tsend.at[i], lax.rem(g + 2 * i, NS)))

    for j in range(SLOTS):
        each_slot(j, lambda j=j: start_halo(0, j))
    each_trans(lambda c: c.start())

    @pl.when(g < STEPS)
    def _():
        for i in range(1, NS):
            mix_copy(i).start()

    def box_copy(i):
        m, far = SENDS[i]
        return pltpu.make_async_remote_copy(
            src_ref=outbox.at[m], dst_ref=inbox.at[i], send_sem=xsem.at[i], recv_sem=xrecv.at[i],
            device_id=(g, lax.rem(q + (NQ + far), NQ)), device_id_type=MESH,
        )

    def send(m):
        for i in range(len(SENDS)):
            if SENDS[i][0] == m:
                pl.when(exists(q + SENDS[i][1]))(lambda i=i: box_copy(i).start())

    send(0)

    def deliver(s, j):
        return pltpu.make_async_remote_copy(
            src_ref=raw.at[s, j], dst_ref=recv.at[first + j],
            send_sem=deliver_sem.at[s, j], recv_sem=recv_sem.at[first + j],
            device_id=(s, q), device_id_type=MESH,
        )

    def deliver_local(s, j):
        return pltpu.make_async_copy(raw.at[s, j], recv.at[first + j], recv_sem.at[first + j])

    def forwards(s):
        return jnp.logical_and(
            jnp.logical_and(core == lax.rem(s, 2), y != s // 2), jnp.logical_and(s >= 1, s < STEPS)
        )

    def forward(s):
        return trans_copy(tall.at[s], s, fsend.at[s], g + 1 - 2 * core)

    def wait_trans(s):
        pltpu.make_async_copy(tall.at[s], tall.at[s], trecv.at[s]).wait()

    def pass_on(s):
        @pl.when(forwards(s))
        def _():
            wait_trans(s)
            forward(s).start()

        each_far_trans(s, lambda c: c.start())

    pass_on(1)

    def tell(i):
        for other in (q + (2 << i), q - (2 << i)):
            @pl.when(exists(other))
            def _():
                pl.semaphore_signal(known.at[i], inc=1, device_id=(g, other), device_id_type=MESH)

    def heard(i):
        count = sum(jnp.where(exists(other), 1, 0) for other in (q + (2 << i), q - (2 << i)))
        pl.semaphore_wait(known.at[i], count)

    tell(0)

    def step(s, carry):
        for i in range(4):
            @pl.when(s == i + 1)
            def _():
                heard(i)
                if i < 3:
                    tell(i + 1)

        @pl.when(jnp.logical_and(g != s, jnp.logical_not(forwards(s))))
        def _():
            wait_trans(s)

        redo = jnp.logical_and(far, lax.rem(s, 2) == 1)

        for d in range(3):
            t = tall[s, d * B:(d + 1) * B, :].T
            if d == 0:
                t = jnp.where(q > 0, t, jnp.zeros_like(t))
            if d == 2:
                t = jnp.where(q < NQ - 1, t, jnp.zeros_like(t))
            tt[d] = t

        def carry_on(parts, turned, tensor):
            parts = [dot(turned[d], parts[d]).astype(BF16) for d in range(3)]
            return dot(jnp.concatenate(parts, axis=1), tensor).astype(BF16)

        for j in range(SLOTS):
            def body(j=j):
                wait_halo(s, j)
                raw[s + 1, j] = carry_on([halo[s, 0, j], raw[s, j], halo[s, 1, j]], tt, tall[s])

                @pl.when(s < STEPS - 1)
                def _():
                    start_halo(s + 1, j)

                @pl.when(g != s + 1)
                def _():
                    deliver(s + 1, j).start()

                @pl.when(g == s + 1)
                def _():
                    deliver_local(s + 1, j).start()

            each_slot(j, body)

        @pl.when(s == 0)
        def _():
            for i in range(2, STEPS):
                pass_on(i)

        @pl.when(redo)
        def _():
            pltpu.make_async_copy(fart.at[s // 2], fart.at[s // 2], ftrecv.at[s // 2]).wait()
            for d in range(3):
                ft[d] = fart[s // 2, d * B:(d + 1) * B, :].T
            for j in range(SLOTS):
                def again(j=j):
                    halo2_copy(s, j).wait_recv()
                    mine, other = raw[s, j], halo2[s // 2, j]
                    low = jnp.where(x_at == 0, other, mine)
                    high = jnp.where(x_at == 0, mine, other)
                    halo[s + 1, side, j] = carry_on([low, halo[s, side, j], high], ft, fart[s // 2])

                each_slot(j, again)

        @pl.when(g != s)
        def _():
            pltpu.make_async_copy(mixall.at[s], mixall.at[s], mrecv.at[s]).wait()

        @pl.when(s < g)
        def _():
            amat[...] = jnp.dot(mixall[s][:, :32], amat[...], precision=lax.Precision.HIGHEST, preferred_element_type=F32)

        return carry

    lax.fori_loop(0, STEPS, step, 0)

    a = amat[...][:, :32].astype(BF16)
    wide = lax.broadcasted_iota(jnp.int32, (KR, 32), 0) // ROWS
    spread = jnp.where(wide == lax.broadcasted_iota(jnp.int32, (KR, 32), 1), 1.0, 0.0).astype(BF16)
    r0 = lax.rem(lax.broadcasted_iota(jnp.int32, (KR, KR), 0), ROWS)
    r1 = lax.rem(lax.broadcasted_iota(jnp.int32, (KR, KR), 1), ROWS)

    def widen(half):
        full = lax.dot_general(half.astype(BF16), spread, (((1,), (1,)), ((), ())), preferred_element_type=F32)
        return jnp.where(r0 == r1, full, 0.0).astype(BF16)

    turned = widen(lax.dot_general(spread, a, (((1,), (1,)), ((), ())), preferred_element_type=F32))
    loads[3].wait()
    for t in range(B // ROWS):
        rows = renv[:, t * ROWS:(t + 1) * ROWS, :].reshape(KR, B)
        mixed = dot(turned, rows).astype(BF16).reshape(WM, ROWS, B)
        for i, w in enumerate(ORDER):
            at = (i % 2) * B + t * ROWS
            renvp[i // 2, at:at + ROWS, :] = mixed[w]
    big = widen(dot(spread, a))

    def pairs(xx, group):
        acc = None
        for p in group:
            pair = jnp.concatenate([recv[ORDER[2 * p]], recv[ORDER[2 * p + 1]]], axis=1)
            term = dot(dot(pair, xx).astype(BF16), renvp[p])
            acc = term if acc is None else acc + term
        return acc

    def twice(x):
        zero = jnp.zeros_like(x)
        return jnp.concatenate([jnp.concatenate([x, zero], axis=1), jnp.concatenate([zero, x], axis=1)], axis=0)

    def apply(x):
        return pairs(twice(x), range(PAIRS)) * mask

    def largest(v):
        return jnp.max(jnp.max(jnp.abs(v), axis=0, keepdims=True), axis=1, keepdims=True)

    def total(v):
        return jnp.sum(jnp.sum(v, axis=0, keepdims=True), axis=1, keepdims=True)

    def log2(v):
        return jnp.log(jnp.maximum(v, 1e-30)) * 1.4426950408889634

    def norm(v, e):
        up = 2.0 * jnp.floor(0.5 * log2(largest(v)) + 0.5)
        return v * jnp.exp2(-up), e + up

    def add(terms):
        top = terms[0][1]
        for _, e in terms[1:]:
            top = jnp.maximum(top, e)
        value = None
        for m, e in terms:
            part = m * jnp.exp2(e - top)
            value = part if value is None else value + part
        return value, top

    def post(m, value, e):
        outbox[m, :B, :] = value
        outbox[m, B:, :] = jnp.broadcast_to(0.5 * e, (AUX, B)).astype(BF16)
        send(m)

    def take(m, far):
        i = SENDS.index((m, far))
        there = exists(q - far)

        @pl.when(there)
        def _():
            box_copy(i).wait_recv()

        value = jnp.where(there, inbox[i, :B, :].astype(F32), 0.0)
        return value, inbox[i, B:, :].astype(F32)[:1, :1]

    def take_scaled(m, far):
        value, e = take(m, far)
        return value, jnp.where(exists(q - far), 2.0 * e, -1000.0)

    def size(m, e):
        return log2(total(m * m)) + 2.0 * e

    x = outbox[0, :B, :]
    xx = twice(x)
    start_l, rank_l = take(0, 1)
    start_r, rank_r = take(0, -1)
    hop = 0.5 * (start_l + start_r)
    acc = None
    for group in GROUPS:
        for p in group:
            for w in ORDER[2 * p:2 * p + 2]:
                pltpu.make_async_copy(recv.at[w], recv.at[w], recv_sem.at[w]).wait()
        part = pairs(xx, group)
        acc = part if acc is None else acc + part
    m1, l1 = norm(mask * (acc + hop), jnp.zeros((1, 1), F32))
    x1 = m1.astype(BF16)
    post(1, x1, l1)
    mp, lp = norm(apply(x1), l1)
    post(2, mp.astype(BF16), lp)
    sizes = [size(m1, l1)]
    half = 0.5 * mask
    half_l = jnp.where(larger < rank_l, 0.5, 0.0).astype(F32)
    half_r = jnp.where(larger < rank_r, 0.5, 0.0).astype(F32)
    m1_l, l1_l = take_scaled(1, 1)
    m1_r, l1_r = take_scaled(1, -1)
    m2, l2 = norm(*add([(mp, lp), (half * m1_l, l1_l), (half * m1_r, l1_r)]))
    r, lr = norm(apply(m2.astype(BF16)), l2)
    sizes.append(size(m2, l2))
    m1_ll, l1_ll = take_scaled(1, 2)
    m1_rr, l1_rr = take_scaled(1, -2)
    mp_l, lp_l = take_scaled(2, 1)
    mp_r, lp_r = take_scaled(2, -1)
    m2_l, l2_l = add([(mp_l, lp_l), (half_l * m1, l1), (half_l * m1_ll, l1_ll)])
    m2_r, l2_r = add([(mp_r, lp_r), (half_r * m1, l1), (half_r * m1_rr, l1_rr)])
    m2_l, l2_l = jnp.where(low_end, 0.0, m2_l), jnp.where(low_end, -1000.0, l2_l)
    m2_r, l2_r = jnp.where(high_end, 0.0, m2_r), jnp.where(high_end, -1000.0, l2_r)
    m3, l3 = norm(*add([(r, lr), (half * m2_l, l2_l), (half * m2_r, l2_r)]))
    x3 = m3.astype(BF16)
    post(3, x3, l3)
    v, lv = norm(apply(x3), l3)
    sizes.append(size(m3, l3))
    for t in range(B // ROWS):
        rows = recv[:, t * ROWS:(t + 1) * ROWS, :].reshape(KR, B)
        env_out[:, t * ROWS:(t + 1) * ROWS, :] = dot(big, rows).astype(BF16).reshape(WM, ROWS, B)
    m3_l, l3_l = take_scaled(3, 1)
    m3_r, l3_r = take_scaled(3, -1)
    m4, l4 = norm(*add([(v, lv), (half * m3_l, l3_l), (half * m3_r, l3_r)]))
    sizes.append(size(m4, l4))

    lane = lax.broadcasted_iota(jnp.int32, (1, B), 1)
    line = jnp.full((1, B), -1e30, F32)
    for k in range(ITERS):
        line = jnp.where(lane == k, sizes[k] + ((ITERS - 1 - k) * LOG_EPS - LOG_N), line)
    psend[...] = line
    pall[q] = line

    def sum_copy(i):
        return pltpu.make_async_remote_copy(
            src_ref=psend, dst_ref=pall.at[q], send_sem=psem, recv_sem=precv,
            device_id=(g, lax.rem(q + i, NQ)), device_id_type=MESH,
        )

    def start_sum(i, carry):
        sum_copy(i).start()
        return carry

    lax.fori_loop(1, NQ, start_sum, 0)

    def drain(s, carry):
        for j in range(SLOTS):
            def body(j=j):
                each_halo(s, j, lambda c: c.wait_send())
                each_halo2(s, j, lambda c: c.wait_send())

                @pl.when(g != s + 1)
                def _():
                    deliver(s + 1, j).wait_send()

            each_slot(j, body)

        @pl.when(forwards(s))
        def _():
            forward(s).wait_send()

        each_far_trans(s, lambda c: c.wait_send())
        return carry

    lax.fori_loop(0, STEPS, drain, 0)
    each_trans(lambda c: c.wait_send())

    @pl.when(g < STEPS)
    def _():
        for i in range(1, NS):
            mix_copy(i).wait_send()

    for i in range(len(SENDS)):
        pl.when(exists(q + SENDS[i][1]))(lambda i=i: box_copy(i).wait_send())
    others = pall.at[pl.ds(0, NQ - 1)]
    pltpu.make_async_copy(others, others, psem).wait()
    pltpu.make_async_copy(others, others, precv).wait()
    logs = pall[...].reshape(NQ, B)
    top = jnp.max(jnp.max(logs, axis=0, keepdims=True), axis=1, keepdims=True)
    top = jnp.maximum(top, ITERS * LOG_EPS)
    square = total(jnp.exp2(logs - top)) + jnp.exp2(ITERS * LOG_EPS - top)
    state[...] = m4 * (jnp.exp2(l4 - 0.5 * top) * lax.rsqrt(square))


def per_device(env_left, transfer, mpo_mix, right_env, start_state, block_rank):
    dma = pltpu.SemaphoreType.DMA
    vmem = pl.BlockSpec(memory_space=pltpu.VMEM)
    hbm = pl.BlockSpec(memory_space=pltpu.HBM)
    state, env = pl.pallas_call(
        kernel,
        out_shape=(
            jax.ShapeDtypeStruct((B, B), F32),
            jax.ShapeDtypeStruct((WM, B, B), BF16),
        ),
        in_specs=[hbm, hbm, hbm, hbm, hbm, pl.BlockSpec(memory_space=pltpu.SMEM)],
        out_specs=(vmem, vmem),
        scratch_shapes=[
            pltpu.VMEM((NS, SLOTS, B, B), BF16),
            pltpu.VMEM((STEPS, 2, SLOTS, B, B), BF16),
            pltpu.VMEM((3, SLOTS, B, B), BF16),
            pltpu.VMEM((3, 3 * B, B), BF16),
            pltpu.VMEM((3, B, B), BF16),
            pltpu.VMEM((WM, B, B), BF16),
            pltpu.VMEM((WM, B, B), BF16),
            pltpu.VMEM((PAIRS, 2 * B, B), BF16),
            pltpu.VMEM((NS, 3 * B, B), BF16),
            pltpu.VMEM((3, B, B), BF16),
            pltpu.VMEM((NS, 32, B), F32),
            pltpu.VMEM((32, B), F32),
            pltpu.VMEM((WM, 1, WM), F32),
            pltpu.VMEM((32, B), F32),
            pltpu.VMEM((B, B), F32),
            pltpu.VMEM((4, MSG, B), BF16),
            pltpu.VMEM((len(SENDS), MSG, B), BF16),
            pltpu.VMEM((1, B), F32),
            pltpu.VMEM((NQ, 1, B), F32),
            dma((SLOTS,)),
            dma((4,)),
            dma((WM,)),
            dma((NS, SLOTS)),
            dma((STEPS, 2, SLOTS)),
            dma((STEPS, 2, SLOTS)),
            dma((3, SLOTS)),
            dma((3, SLOTS)),
            dma((3,)),
            dma((3, 2)),
            dma((NS,)),
            dma((NS,)),
            dma((NS,)),
            dma((NS,)),
            dma((NS,)),
            dma((len(SENDS),)),
            dma((len(SENDS),)),
            dma,
            dma,
            pltpu.SemaphoreType.REGULAR((4,)),
        ],
        compiler_params=pltpu.CompilerParams(
            collective_id=0, has_side_effects=True, vmem_limit_bytes=40 * 1024 * 1024
        ),
    )(
        *(
            pltpu.with_memory_space_constraint(value, pltpu.HBM)
            for value in (
                env_left.reshape(WM, B, B),
                transfer.reshape(3 * B, B),
                jnp.transpose(mpo_mix, (1, 0, 2)),
                right_env.reshape(WM, B, B),
                start_state.reshape(B, B),
            )
        ),
        block_rank,
    )
    return state.reshape(1, 1, B, B), env.reshape(1, WM, 1, B, B)


def solution(mesh):
    in_specs = (
        P(None, "blk", None, None),
        P("sec", "blk", None, None, None),
        P("sec", None, None),
        P("sec", None, "blk", None, None),
        P("sec", "blk", None, None),
        P("blk"),
    )
    out_specs = (P("sec", "blk", None, None), P("sec", None, "blk", None, None))
    return jax.shard_map(
        per_device, mesh=mesh, in_specs=in_specs, out_specs=out_specs, check_vma=False
    )
```

```python
import jax
import jax.numpy as jnp
from jax import lax
from jax.experimental import pallas as pl
from jax.experimental.pallas import tpu as pltpu
from jax.sharding import PartitionSpec as P

ITERS = 4
B = 128
WM = 26
NS = 8
NQ = 32
NX = 4
NEAR = (1, -1, 2, -2)
SLOTS = 4
STEPS = NS - 1
PAIRS = WM // 2
ROWS = 16
KR = WM * ROWS
FIRSTS = (0, 4, 7, 11, 14, 17, 20, 23)
ORDER = [f + j for j in range(3) for f in FIRSTS] + [3, 10]
GROUPS = (range(0, 8), range(8, 13))
AUX = 16
MSG = B + AUX
SENDS = ((0, 1), (0, -1), (1, 2), (1, -2), (1, 1), (1, -1), (2, 1), (2, -1), (3, 1), (3, -1))
LOG_EPS = -19.931568569324174
LOG_N = 19.0
MESH = pl.DeviceIdType.MESH
F32 = jnp.float32
BF16 = jnp.bfloat16


def dot(a, b):
    return jnp.dot(a, b, preferred_element_type=F32)


def kernel(
    env_hbm, trans_hbm, mix_hbm, renv_hbm, start_hbm, rank, state, env_out,
    raw, halo, halo2, fart, ft, recv, renv, renvp, tall, tt, mixall, amat, mix_in, own_mix,
    start, outbox, inbox, psend, pall,
    load_sem, in_sem, recv_sem, deliver_sem,
    hrecv, hsend, h2recv, h2send, ftrecv, ftsend, trecv, tsend, fsend, mrecv, msend,
    xrecv, xsem, precv, psem, known,
):
    g = lax.axis_index("sec")
    q = lax.axis_index("blk")
    y = g // 2
    core = lax.rem(g, 2)
    right = lax.rem(q + 1, NQ)
    left = lax.rem(q + NQ - 1, NQ)
    first = 3 * g + jnp.where(g >= 1, 1, 0) + jnp.where(g >= 3, 1, 0)
    four = jnp.logical_or(g == 0, g == 2)
    x_at = lax.rem(q, NX)
    low_end, high_end = q == 0, q == NQ - 1
    at_low = jnp.logical_and(x_at == 0, jnp.logical_not(low_end))
    at_high = jnp.logical_and(x_at == NX - 1, jnp.logical_not(high_end))
    far = jnp.logical_or(at_low, at_high)
    gives = jnp.logical_or(jnp.logical_and(x_at == 1, q > NX), jnp.logical_and(x_at == 2, q < NQ - NX))

    def exists(other):
        return jnp.logical_and(other >= 0, other < NQ)

    side = jnp.where(x_at == 0, 0, 1)
    beyond = jnp.where(x_at == 0, left, right)
    two_off = lax.rem(jnp.where(x_at == 2, q + 2, q + (NQ - 2)), NQ)

    barrier = pltpu.get_barrier_semaphore()

    def greet_sec(i, carry):
        pl.semaphore_signal(barrier, inc=1, device_id=(lax.rem(g + i, NS), q), device_id_type=MESH)
        return carry

    lax.fori_loop(1, NS, greet_sec, 0)
    greeted = NS - 1 + jnp.where(jnp.logical_and(far, core == 1), 1, 0)
    for i in NEAR:
        @pl.when(exists(q + i))
        def _():
            pl.semaphore_signal(barrier, inc=1, device_id=(g, q + i), device_id_type=MESH)

        greeted += jnp.where(exists(q + i), 1, 0)

    @pl.when(jnp.logical_and(far, core == 0))
    def _():
        pl.semaphore_signal(barrier, inc=1, device_id=(g + 1, beyond), device_id_type=MESH)


    loads = [
        pltpu.make_async_copy(trans_hbm, tall.at[g], in_sem.at[0]),
        pltpu.make_async_copy(mix_hbm, mix_in, in_sem.at[1]),
        pltpu.make_async_copy(start_hbm, start, in_sem.at[2]),
        pltpu.make_async_copy(renv_hbm, renv, in_sem.at[3]),
    ]

    def each_slot(j, body):
        if j < SLOTS - 1:
            body()
        else:
            pl.when(four)(body)

    def load(j):
        return pltpu.make_async_copy(env_hbm.at[first + j], raw.at[0, j], load_sem.at[j])

    loads[0].start()
    for j in range(SLOTS):
        each_slot(j, lambda j=j: load(j).start())
    for c in loads[1:]:
        c.start()

    @pl.when(g == 0)
    def _():
        def body(w, carry):
            pltpu.make_async_copy(env_hbm.at[w], recv.at[w], recv_sem.at[w]).start()
            return carry

        lax.fori_loop(0, WM, body, 0)

    own_mix[...] = jnp.zeros_like(own_mix)
    for end, at in ((low_end, 0), (high_end, 1)):
        @pl.when(end)
        def _():
            def clear(s, carry):
                halo[s, at] = jnp.zeros((SLOTS, B, B), BF16)
                return carry

            lax.fori_loop(0, STEPS, clear, 0)

    loads[1].wait()
    own_mix[:WM, :WM] = mix_in[...].reshape(WM, WM)
    mixall[g] = own_mix[...]
    row = lax.broadcasted_iota(jnp.int32, (32, B), 0)
    col = lax.broadcasted_iota(jnp.int32, (32, B), 1)
    amat[...] = jnp.where(row == col, 1.0, 0.0).astype(F32)
    keep0 = lax.broadcasted_iota(jnp.int32, (B, B), 0)
    keep1 = lax.broadcasted_iota(jnp.int32, (B, B), 1)
    larger = jnp.maximum(keep0, keep1).astype(F32)
    my_rank = rank[0].astype(F32)
    mask = jnp.where(larger < my_rank, 1.0, 0.0).astype(F32)
    loads[2].wait()
    outbox[0, :B, :] = (start[...] * mask).astype(BF16)
    outbox[0, B:, :] = jnp.full((AUX, B), my_rank, F32).astype(BF16)
    loads[0].wait()
    for j in range(SLOTS):
        each_slot(j, lambda j=j: load(j).wait())

    pl.semaphore_wait(barrier, greeted)

    def crossed(s):
        return jnp.logical_or(s == 0, lax.rem(s, 2) == 1)

    def halo_copy(s, j, to):
        return pltpu.make_async_remote_copy(
            src_ref=raw.at[s, j], dst_ref=halo.at[s, 1 - to, j],
            send_sem=hsend.at[s, to, j], recv_sem=hrecv.at[s, 1 - to, j],
            device_id=(g, right if to else left), device_id_type=MESH,
        )

    def meets(to, s):
        end, at = (high_end, at_high) if to else (low_end, at_low)
        return jnp.logical_and(jnp.logical_not(end), jnp.logical_or(jnp.logical_not(at), crossed(s)))

    def each_halo(s, j, act):
        for to in range(2):
            pl.when(meets(to, s))(lambda to=to: act(halo_copy(s, j, to)))

    def wait_halo(s, j):
        for at in range(2):
            @pl.when(meets(at, s))
            def _():
                halo_copy(s, j, 1 - at).wait_recv()

    def halo2_copy(s, j):
        return pltpu.make_async_remote_copy(
            src_ref=raw.at[s, j], dst_ref=halo2.at[s // 2, j],
            send_sem=h2send.at[s // 2, j], recv_sem=h2recv.at[s // 2, j],
            device_id=(g, two_off), device_id_type=MESH,
        )

    def each_halo2(s, j, act):
        pl.when(jnp.logical_and(gives, lax.rem(s, 2) == 1))(lambda: act(halo2_copy(s, j)))

    def start_halo(s, j):
        each_halo(s, j, lambda c: c.start())
        each_halo2(s, j, lambda c: c.start())

    def far_trans(s, i):
        return pltpu.make_async_remote_copy(
            src_ref=tall.at[s], dst_ref=fart.at[s // 2],
            send_sem=ftsend.at[s // 2, i], recv_sem=ftrecv.at[s // 2],
            device_id=(g - i, beyond), device_id_type=MESH,
        )

    def each_far_trans(s, act):
        @pl.when(jnp.logical_and(jnp.logical_and(far, core == 1), jnp.logical_and(lax.rem(s, 2) == 1, s < STEPS)))
        def _():
            for i in range(2):
                act(far_trans(s, i))

    def trans_copy(src, s, sem, other):
        return pltpu.make_async_remote_copy(
            src_ref=src, dst_ref=tall.at[s], send_sem=sem, recv_sem=trecv.at[s],
            device_id=(other, q), device_id_type=MESH,
        )

    def mix_copy(i):
        return pltpu.make_async_remote_copy(
            src_ref=own_mix, dst_ref=mixall.at[g], send_sem=msend.at[i], recv_sem=mrecv.at[g],
            device_id=(lax.rem(g + i, NS), q), device_id_type=MESH,
        )

    def each_trans(act):
        @pl.when(g == 0)
        def _():
            for i in range(1, NS):
                act(trans_copy(tall.at[g], 0, tsend.at[i], i))

        @pl.when(jnp.logical_and(g > 0, g < STEPS))
        def _():
            act(trans_copy(tall.at[g], g, tsend.at[0], g + 1 - 2 * core))
            for i in range(1, 4):
                act(trans_copy(tall.at[g], g, tsend.at[i], lax.rem(g + 2 * i, NS)))

    for j in range(SLOTS):
        each_slot(j, lambda j=j: start_halo(0, j))
    each_trans(lambda c: c.start())

    def box_copy(i):
        m, far = SENDS[i]
        return pltpu.make_async_remote_copy(
            src_ref=outbox.at[m], dst_ref=inbox.at[i], send_sem=xsem.at[i], recv_sem=xrecv.at[i],
            device_id=(g, lax.rem(q + (NQ + far), NQ)), device_id_type=MESH,
        )

    def send(m):
        for i in range(len(SENDS)):
            if SENDS[i][0] == m:
                pl.when(exists(q + SENDS[i][1]))(lambda i=i: box_copy(i).start())

    send(0)

    def deliver(s, j):
        return pltpu.make_async_remote_copy(
            src_ref=raw.at[s, j], dst_ref=recv.at[first + j],
            send_sem=deliver_sem.at[s, j], recv_sem=recv_sem.at[first + j],
            device_id=(s, q), device_id_type=MESH,
        )

    def deliver_local(s, j):
        return pltpu.make_async_copy(raw.at[s, j], recv.at[first + j], recv_sem.at[first + j])

    def forwards(s):
        return jnp.logical_and(
            jnp.logical_and(core == lax.rem(s, 2), y != s // 2), jnp.logical_and(s >= 1, s < STEPS)
        )

    def forward(s):
        return trans_copy(tall.at[s], s, fsend.at[s], g + 1 - 2 * core)

    def wait_trans(s):
        pltpu.make_async_copy(tall.at[s], tall.at[s], trecv.at[s]).wait()

    def pass_on(s):
        @pl.when(forwards(s))
        def _():
            wait_trans(s)
            forward(s).start()

        each_far_trans(s, lambda c: c.start())

    pass_on(1)

    def tell(i):
        for other in (q + (2 << i), q - (2 << i)):
            @pl.when(exists(other))
            def _():
                pl.semaphore_signal(known.at[i], inc=1, device_id=(g, other), device_id_type=MESH)

    def heard(i):
        count = sum(jnp.where(exists(other), 1, 0) for other in (q + (2 << i), q - (2 << i)))
        pl.semaphore_wait(known.at[i], count)

    tell(0)

    def multiply(s):
        @pl.when(g != s)
        def _():
            pltpu.make_async_copy(mixall.at[s], mixall.at[s], mrecv.at[s]).wait()

        @pl.when(s < g)
        def _():
            amat[...] = jnp.dot(mixall[s][:, :32], amat[...], precision=lax.Precision.HIGHEST, preferred_element_type=F32)


    def step(s, carry):
        for i in range(4):
            @pl.when(s == i + 1)
            def _():
                heard(i)
                if i < 3:
                    tell(i + 1)

        @pl.when(jnp.logical_and(g != s, jnp.logical_not(forwards(s))))
        def _():
            wait_trans(s)

        redo = jnp.logical_and(far, lax.rem(s, 2) == 1)

        for d in range(3):
            t = tall[s, d * B:(d + 1) * B, :].T
            if d == 0:
                t = jnp.where(q > 0, t, jnp.zeros_like(t))
            if d == 2:
                t = jnp.where(q < NQ - 1, t, jnp.zeros_like(t))
            tt[d] = t

        def carry_on(parts, turned, tensor):
            parts = [dot(turned[d], parts[d]).astype(BF16) for d in range(3)]
            return dot(jnp.concatenate(parts, axis=1), tensor).astype(BF16)

        for j in range(SLOTS):
            def body(j=j):
                wait_halo(s, j)
                raw[s + 1, j] = carry_on([halo[s, 0, j], raw[s, j], halo[s, 1, j]], tt, tall[s])

                @pl.when(s < STEPS - 1)
                def _():
                    start_halo(s + 1, j)

                @pl.when(g != s + 1)
                def _():
                    deliver(s + 1, j).start()

                @pl.when(g == s + 1)
                def _():
                    deliver_local(s + 1, j).start()

            each_slot(j, body)

        @pl.when(s == 0)
        def _():
            for i in range(2, STEPS):
                pass_on(i)

            @pl.when(g < STEPS)
            def _():
                for i in range(1, NS):
                    mix_copy(i).start()

        @pl.when(redo)
        def _():
            pltpu.make_async_copy(fart.at[s // 2], fart.at[s // 2], ftrecv.at[s // 2]).wait()
            for d in range(3):
                ft[d] = fart[s // 2, d * B:(d + 1) * B, :].T
            for j in range(SLOTS):
                def again(j=j):
                    halo2_copy(s, j).wait_recv()
                    mine, other = raw[s, j], halo2[s // 2, j]
                    low = jnp.where(x_at == 0, other, mine)
                    high = jnp.where(x_at == 0, mine, other)
                    halo[s + 1, side, j] = carry_on([low, halo[s, side, j], high], ft, fart[s // 2])

                each_slot(j, again)

        pl.when(s >= 3)(lambda: multiply(s - 3))
        return carry

    lax.fori_loop(0, STEPS, step, 0)
    for s in range(STEPS - 3, STEPS):
        multiply(s)

    a = amat[...][:, :32].astype(BF16)
    wide = lax.broadcasted_iota(jnp.int32, (KR, 32), 0) // ROWS
    spread = jnp.where(wide == lax.broadcasted_iota(jnp.int32, (KR, 32), 1), 1.0, 0.0).astype(BF16)
    r0 = lax.rem(lax.broadcasted_iota(jnp.int32, (KR, KR), 0), ROWS)
    r1 = lax.rem(lax.broadcasted_iota(jnp.int32, (KR, KR), 1), ROWS)

    def widen(half):
        full = lax.dot_general(half.astype(BF16), spread, (((1,), (1,)), ((), ())), preferred_element_type=F32)
        return jnp.where(r0 == r1, full, 0.0).astype(BF16)

    turned = widen(lax.dot_general(spread, a, (((1,), (1,)), ((), ())), preferred_element_type=F32))
    loads[3].wait()
    for t in range(B // ROWS):
        rows = renv[:, t * ROWS:(t + 1) * ROWS, :].reshape(KR, B)
        mixed = dot(turned, rows).astype(BF16).reshape(WM, ROWS, B)
        for i, w in enumerate(ORDER):
            at = (i % 2) * B + t * ROWS
            renvp[i // 2, at:at + ROWS, :] = mixed[w]
    big = widen(dot(spread, a))

    def pairs(xx, group):
        acc = None
        for p in group:
            pair = jnp.concatenate([recv[ORDER[2 * p]], recv[ORDER[2 * p + 1]]], axis=1)
            term = dot(dot(pair, xx).astype(BF16), renvp[p])
            acc = term if acc is None else acc + term
        return acc

    def twice(x):
        zero = jnp.zeros_like(x)
        return jnp.concatenate([jnp.concatenate([x, zero], axis=1), jnp.concatenate([zero, x], axis=1)], axis=0)

    def apply(x):
        return pairs(twice(x), range(PAIRS)) * mask

    def largest(v):
        return jnp.max(jnp.max(jnp.abs(v), axis=0, keepdims=True), axis=1, keepdims=True)

    def total(v):
        return jnp.sum(jnp.sum(v, axis=0, keepdims=True), axis=1, keepdims=True)

    def log2(v):
        return jnp.log(jnp.maximum(v, 1e-30)) * 1.4426950408889634

    def norm(v, e):
        up = 2.0 * jnp.floor(0.5 * log2(largest(v)) + 0.5)
        return v * jnp.exp2(-up), e + up

    def add(terms):
        top = terms[0][1]
        for _, e in terms[1:]:
            top = jnp.maximum(top, e)
        value = None
        for m, e in terms:
            part = m * jnp.exp2(e - top)
            value = part if value is None else value + part
        return value, top

    def post(m, value, e):
        outbox[m, :B, :] = value
        outbox[m, B:, :] = jnp.broadcast_to(0.5 * e, (AUX, B)).astype(BF16)
        send(m)

    def take(m, far):
        i = SENDS.index((m, far))
        there = exists(q - far)

        @pl.when(there)
        def _():
            box_copy(i).wait_recv()

        value = jnp.where(there, inbox[i, :B, :].astype(F32), 0.0)
        return value, inbox[i, B:, :].astype(F32)[:1, :1]

    def take_scaled(m, far):
        value, e = take(m, far)
        return value, jnp.where(exists(q - far), 2.0 * e, -1000.0)

    def size(m, e):
        return log2(total(m * m)) + 2.0 * e

    x = outbox[0, :B, :]
    xx = twice(x)
    start_l, rank_l = take(0, 1)
    start_r, rank_r = take(0, -1)
    hop = 0.5 * (start_l + start_r)
    acc = None
    for group in GROUPS:
        for p in group:
            for w in ORDER[2 * p:2 * p + 2]:
                pltpu.make_async_copy(recv.at[w], recv.at[w], recv_sem.at[w]).wait()
        part = pairs(xx, group)
        acc = part if acc is None else acc + part
    m1, l1 = norm(mask * (acc + hop), jnp.zeros((1, 1), F32))
    x1 = m1.astype(BF16)
    post(1, x1, l1)
    mp, lp = norm(apply(x1), l1)
    post(2, mp.astype(BF16), lp)
    sizes = [size(m1, l1)]
    half = 0.5 * mask
    half_l = jnp.where(larger < rank_l, 0.5, 0.0).astype(F32)
    half_r = jnp.where(larger < rank_r, 0.5, 0.0).astype(F32)
    m1_l, l1_l = take_scaled(1, 1)
    m1_r, l1_r = take_scaled(1, -1)
    m2, l2 = norm(*add([(mp, lp), (half * m1_l, l1_l), (half * m1_r, l1_r)]))
    r, lr = norm(apply(m2.astype(BF16)), l2)
    sizes.append(size(m2, l2))
    m1_ll, l1_ll = take_scaled(1, 2)
    m1_rr, l1_rr = take_scaled(1, -2)
    mp_l, lp_l = take_scaled(2, 1)
    mp_r, lp_r = take_scaled(2, -1)
    m2_l, l2_l = add([(mp_l, lp_l), (half_l * m1, l1), (half_l * m1_ll, l1_ll)])
    m2_r, l2_r = add([(mp_r, lp_r), (half_r * m1, l1), (half_r * m1_rr, l1_rr)])
    m2_l, l2_l = jnp.where(low_end, 0.0, m2_l), jnp.where(low_end, -1000.0, l2_l)
    m2_r, l2_r = jnp.where(high_end, 0.0, m2_r), jnp.where(high_end, -1000.0, l2_r)
    m3, l3 = norm(*add([(r, lr), (half * m2_l, l2_l), (half * m2_r, l2_r)]))
    x3 = m3.astype(BF16)
    post(3, x3, l3)
    v, lv = norm(apply(x3), l3)
    sizes.append(size(m3, l3))
    for t in range(B // ROWS):
        rows = recv[:, t * ROWS:(t + 1) * ROWS, :].reshape(KR, B)
        env_out[:, t * ROWS:(t + 1) * ROWS, :] = dot(big, rows).astype(BF16).reshape(WM, ROWS, B)
    m3_l, l3_l = take_scaled(3, 1)
    m3_r, l3_r = take_scaled(3, -1)
    m4, l4 = norm(*add([(v, lv), (half * m3_l, l3_l), (half * m3_r, l3_r)]))
    sizes.append(size(m4, l4))

    lane = lax.broadcasted_iota(jnp.int32, (1, B), 1)
    line = jnp.full((1, B), -1e30, F32)
    for k in range(ITERS):
        line = jnp.where(lane == k, sizes[k] + ((ITERS - 1 - k) * LOG_EPS - LOG_N), line)
    psend[...] = line
    pall[q] = line

    def sum_copy(i):
        return pltpu.make_async_remote_copy(
            src_ref=psend, dst_ref=pall.at[q], send_sem=psem, recv_sem=precv,
            device_id=(g, lax.rem(q + i, NQ)), device_id_type=MESH,
        )

    def start_sum(i, carry):
        sum_copy(i).start()
        return carry

    lax.fori_loop(1, NQ, start_sum, 0)

    def drain(s, carry):
        for j in range(SLOTS):
            def body(j=j):
                each_halo(s, j, lambda c: c.wait_send())
                each_halo2(s, j, lambda c: c.wait_send())

                @pl.when(g != s + 1)
                def _():
                    deliver(s + 1, j).wait_send()

            each_slot(j, body)

        @pl.when(forwards(s))
        def _():
            forward(s).wait_send()

        each_far_trans(s, lambda c: c.wait_send())
        return carry

    lax.fori_loop(0, STEPS, drain, 0)
    each_trans(lambda c: c.wait_send())

    @pl.when(g < STEPS)
    def _():
        for i in range(1, NS):
            mix_copy(i).wait_send()

    for i in range(len(SENDS)):
        pl.when(exists(q + SENDS[i][1]))(lambda i=i: box_copy(i).wait_send())
    others = pall.at[pl.ds(0, NQ - 1)]
    pltpu.make_async_copy(others, others, psem).wait()
    pltpu.make_async_copy(others, others, precv).wait()
    logs = pall[...].reshape(NQ, B)
    top = jnp.max(jnp.max(logs, axis=0, keepdims=True), axis=1, keepdims=True)
    top = jnp.maximum(top, ITERS * LOG_EPS)
    square = total(jnp.exp2(logs - top)) + jnp.exp2(ITERS * LOG_EPS - top)
    state[...] = m4 * (jnp.exp2(l4 - 0.5 * top) * lax.rsqrt(square))


def per_device(env_left, transfer, mpo_mix, right_env, start_state, block_rank):
    dma = pltpu.SemaphoreType.DMA
    vmem = pl.BlockSpec(memory_space=pltpu.VMEM)
    hbm = pl.BlockSpec(memory_space=pltpu.HBM)
    state, env = pl.pallas_call(
        kernel,
        out_shape=(
            jax.ShapeDtypeStruct((B, B), F32),
            jax.ShapeDtypeStruct((WM, B, B), BF16),
        ),
        in_specs=[hbm, hbm, hbm, hbm, hbm, pl.BlockSpec(memory_space=pltpu.SMEM)],
        out_specs=(vmem, vmem),
        scratch_shapes=[
            pltpu.VMEM((NS, SLOTS, B, B), BF16),
            pltpu.VMEM((STEPS, 2, SLOTS, B, B), BF16),
            pltpu.VMEM((3, SLOTS, B, B), BF16),
            pltpu.VMEM((3, 3 * B, B), BF16),
            pltpu.VMEM((3, B, B), BF16),
            pltpu.VMEM((WM, B, B), BF16),
            pltpu.VMEM((WM, B, B), BF16),
            pltpu.VMEM((PAIRS, 2 * B, B), BF16),
            pltpu.VMEM((NS, 3 * B, B), BF16),
            pltpu.VMEM((3, B, B), BF16),
            pltpu.VMEM((NS, 32, B), F32),
            pltpu.VMEM((32, B), F32),
            pltpu.VMEM((WM, 1, WM), F32),
            pltpu.VMEM((32, B), F32),
            pltpu.VMEM((B, B), F32),
            pltpu.VMEM((4, MSG, B), BF16),
            pltpu.VMEM((len(SENDS), MSG, B), BF16),
            pltpu.VMEM((1, B), F32),
            pltpu.VMEM((NQ, 1, B), F32),
            dma((SLOTS,)),
            dma((4,)),
            dma((WM,)),
            dma((NS, SLOTS)),
            dma((STEPS, 2, SLOTS)),
            dma((STEPS, 2, SLOTS)),
            dma((3, SLOTS)),
            dma((3, SLOTS)),
            dma((3,)),
            dma((3, 2)),
            dma((NS,)),
            dma((NS,)),
            dma((NS,)),
            dma((NS,)),
            dma((NS,)),
            dma((len(SENDS),)),
            dma((len(SENDS),)),
            dma,
            dma,
            pltpu.SemaphoreType.REGULAR((4,)),
        ],
        compiler_params=pltpu.CompilerParams(
            collective_id=0, has_side_effects=True, vmem_limit_bytes=40 * 1024 * 1024
        ),
    )(
        *(
            pltpu.with_memory_space_constraint(value, pltpu.HBM)
            for value in (
                env_left.reshape(WM, B, B),
                transfer.reshape(3 * B, B),
                jnp.transpose(mpo_mix, (1, 0, 2)),
                right_env.reshape(WM, B, B),
                start_state.reshape(B, B),
            )
        ),
        block_rank,
    )
    return state.reshape(1, 1, B, B), env.reshape(1, WM, 1, B, B)


def solution(mesh):
    in_specs = (
        P(None, "blk", None, None),
        P("sec", "blk", None, None, None),
        P("sec", None, None),
        P("sec", None, "blk", None, None),
        P("sec", "blk", None, None),
        P("blk"),
    )
    out_specs = (P("sec", "blk", None, None), P("sec", None, "blk", None, None))
    return jax.shard_map(
        per_device, mesh=mesh, in_specs=in_specs, out_specs=out_specs, check_vma=False
    )
```

```python
import jax
import jax.numpy as jnp
from jax import lax
from jax.experimental import pallas as pl
from jax.experimental.pallas import tpu as pltpu
from jax.sharding import PartitionSpec as P

ITERS = 4
B = 128
WM = 26
NS = 8
NQ = 32
NX = 4
NEAR = (1, -1, 2, -2)
SLOTS = 4
STEPS = NS - 1
PAIRS = WM // 2
ROWS = 16
KR = WM * ROWS
FIRSTS = (0, 4, 7, 11, 14, 17, 20, 23)
ORDER = [f + j for j in range(3) for f in FIRSTS] + [3, 10]
GROUPS = (range(0, 13),)
AUX = 16
MSG = B + AUX
SENDS = ((0, 1), (0, -1), (1, 2), (1, -2), (1, 1), (1, -1), (2, 1), (2, -1), (3, 1), (3, -1))
LOG_EPS = -19.931568569324174
LOG_N = 19.0
MESH = pl.DeviceIdType.MESH
F32 = jnp.float32
BF16 = jnp.bfloat16


def dot(a, b):
    return jnp.dot(a, b, preferred_element_type=F32)


def kernel(
    env_hbm, trans_hbm, mix_hbm, renv_hbm, start_hbm, rank, state, env_out,
    raw, halo, halo2, fart, ft, recv, renv, renvp, tall, tt, mixall, amat, mix_in, own_mix,
    start, outbox, inbox, psend, pall,
    load_sem, in_sem, recv_sem, deliver_sem,
    hrecv, hsend, h2recv, h2send, ftrecv, ftsend, trecv, tsend, fsend, mrecv, msend,
    xrecv, xsem, precv, psem, known,
):
    g = lax.axis_index("sec")
    q = lax.axis_index("blk")
    y = g // 2
    core = lax.rem(g, 2)
    right = lax.rem(q + 1, NQ)
    left = lax.rem(q + NQ - 1, NQ)
    first = 3 * g + jnp.where(g >= 1, 1, 0) + jnp.where(g >= 3, 1, 0)
    four = jnp.logical_or(g == 0, g == 2)
    x_at = lax.rem(q, NX)
    low_end, high_end = q == 0, q == NQ - 1
    at_low = jnp.logical_and(x_at == 0, jnp.logical_not(low_end))
    at_high = jnp.logical_and(x_at == NX - 1, jnp.logical_not(high_end))
    far = jnp.logical_or(at_low, at_high)
    gives = jnp.logical_or(jnp.logical_and(x_at == 1, q > NX), jnp.logical_and(x_at == 2, q < NQ - NX))

    def exists(other):
        return jnp.logical_and(other >= 0, other < NQ)

    side = jnp.where(x_at == 0, 0, 1)
    beyond = jnp.where(x_at == 0, left, right)
    two_off = lax.rem(jnp.where(x_at == 2, q + 2, q + (NQ - 2)), NQ)

    barrier = pltpu.get_barrier_semaphore()

    def greet_sec(i, carry):
        pl.semaphore_signal(barrier, inc=1, device_id=(lax.rem(g + i, NS), q), device_id_type=MESH)
        return carry

    lax.fori_loop(1, NS, greet_sec, 0)
    greeted = NS - 1 + jnp.where(jnp.logical_and(far, core == 1), 1, 0)
    for i in NEAR:
        @pl.when(exists(q + i))
        def _():
            pl.semaphore_signal(barrier, inc=1, device_id=(g, q + i), device_id_type=MESH)

        greeted += jnp.where(exists(q + i), 1, 0)

    @pl.when(jnp.logical_and(far, core == 0))
    def _():
        pl.semaphore_signal(barrier, inc=1, device_id=(g + 1, beyond), device_id_type=MESH)


    loads = [
        pltpu.make_async_copy(trans_hbm, tall.at[g], in_sem.at[0]),
        pltpu.make_async_copy(mix_hbm, mix_in, in_sem.at[1]),
        pltpu.make_async_copy(start_hbm, start, in_sem.at[2]),
        pltpu.make_async_copy(renv_hbm, renv, in_sem.at[3]),
    ]

    def each_slot(j, body):
        if j < SLOTS - 1:
            body()
        else:
            pl.when(four)(body)

    def load(j):
        return pltpu.make_async_copy(env_hbm.at[first + j], raw.at[0, j], load_sem.at[j])

    loads[0].start()
    for j in range(SLOTS):
        each_slot(j, lambda j=j: load(j).start())
    for c in loads[1:]:
        c.start()

    @pl.when(g == 0)
    def _():
        def body(w, carry):
            pltpu.make_async_copy(env_hbm.at[w], recv.at[w], recv_sem.at[w]).start()
            return carry

        lax.fori_loop(0, WM, body, 0)

    own_mix[...] = jnp.zeros_like(own_mix)
    for end, at in ((low_end, 0), (high_end, 1)):
        @pl.when(end)
        def _():
            def clear(s, carry):
                halo[s, at] = jnp.zeros((SLOTS, B, B), BF16)
                return carry

            lax.fori_loop(0, STEPS, clear, 0)

    loads[1].wait()
    own_mix[:WM, :WM] = mix_in[...].reshape(WM, WM)
    mixall[g] = own_mix[...]
    row = lax.broadcasted_iota(jnp.int32, (32, B), 0)
    col = lax.broadcasted_iota(jnp.int32, (32, B), 1)
    amat[...] = jnp.where(row == col, 1.0, 0.0).astype(F32)
    keep0 = lax.broadcasted_iota(jnp.int32, (B, B), 0)
    keep1 = lax.broadcasted_iota(jnp.int32, (B, B), 1)
    larger = jnp.maximum(keep0, keep1).astype(F32)
    my_rank = rank[0].astype(F32)
    mask = jnp.where(larger < my_rank, 1.0, 0.0).astype(F32)
    loads[2].wait()
    outbox[0, :B, :] = (start[...] * mask).astype(BF16)
    outbox[0, B:, :] = jnp.full((AUX, B), my_rank, F32).astype(BF16)
    loads[0].wait()
    for j in range(SLOTS):
        each_slot(j, lambda j=j: load(j).wait())

    pl.semaphore_wait(barrier, greeted)

    def crossed(s):
        return jnp.logical_or(s == 0, lax.rem(s, 2) == 1)

    def halo_copy(s, j, to):
        return pltpu.make_async_remote_copy(
            src_ref=raw.at[s, j], dst_ref=halo.at[s, 1 - to, j],
            send_sem=hsend.at[s, to, j], recv_sem=hrecv.at[s, 1 - to, j],
            device_id=(g, right if to else left), device_id_type=MESH,
        )

    def meets(to, s):
        end, at = (high_end, at_high) if to else (low_end, at_low)
        return jnp.logical_and(jnp.logical_not(end), jnp.logical_or(jnp.logical_not(at), crossed(s)))

    def each_halo(s, j, act):
        for to in range(2):
            pl.when(meets(to, s))(lambda to=to: act(halo_copy(s, j, to)))

    def wait_halo(s, j):
        for at in range(2):
            @pl.when(meets(at, s))
            def _():
                halo_copy(s, j, 1 - at).wait_recv()

    def halo2_copy(s, j):
        return pltpu.make_async_remote_copy(
            src_ref=raw.at[s, j], dst_ref=halo2.at[s // 2, j],
            send_sem=h2send.at[s // 2, j], recv_sem=h2recv.at[s // 2, j],
            device_id=(g, two_off), device_id_type=MESH,
        )

    def each_halo2(s, j, act):
        pl.when(jnp.logical_and(gives, lax.rem(s, 2) == 1))(lambda: act(halo2_copy(s, j)))

    def start_halo(s, j):
        each_halo(s, j, lambda c: c.start())
        each_halo2(s, j, lambda c: c.start())

    def far_trans(s, i):
        return pltpu.make_async_remote_copy(
            src_ref=tall.at[s], dst_ref=fart.at[s // 2],
            send_sem=ftsend.at[s // 2, i], recv_sem=ftrecv.at[s // 2],
            device_id=(g - i, beyond), device_id_type=MESH,
        )

    def each_far_trans(s, act):
        @pl.when(jnp.logical_and(jnp.logical_and(far, core == 1), jnp.logical_and(lax.rem(s, 2) == 1, s < STEPS)))
        def _():
            for i in range(2):
                act(far_trans(s, i))

    def trans_copy(src, s, sem, other):
        return pltpu.make_async_remote_copy(
            src_ref=src, dst_ref=tall.at[s], send_sem=sem, recv_sem=trecv.at[s],
            device_id=(other, q), device_id_type=MESH,
        )

    def mix_copy(i):
        return pltpu.make_async_remote_copy(
            src_ref=own_mix, dst_ref=mixall.at[g], send_sem=msend.at[i], recv_sem=mrecv.at[g],
            device_id=(lax.rem(g + i, NS), q), device_id_type=MESH,
        )

    def each_trans(act):
        @pl.when(g == 0)
        def _():
            for i in range(1, NS):
                act(trans_copy(tall.at[g], 0, tsend.at[i], i))

        @pl.when(jnp.logical_and(g > 0, g < STEPS))
        def _():
            act(trans_copy(tall.at[g], g, tsend.at[0], g + 1 - 2 * core))
            for i in range(1, 4):
                act(trans_copy(tall.at[g], g, tsend.at[i], lax.rem(g + 2 * i, NS)))

    for j in range(SLOTS):
        each_slot(j, lambda j=j: start_halo(0, j))
    each_trans(lambda c: c.start())

    def box_copy(i):
        m, far = SENDS[i]
        return pltpu.make_async_remote_copy(
            src_ref=outbox.at[m], dst_ref=inbox.at[i], send_sem=xsem.at[i], recv_sem=xrecv.at[i],
            device_id=(g, lax.rem(q + (NQ + far), NQ)), device_id_type=MESH,
        )

    def send(m):
        for i in range(len(SENDS)):
            if SENDS[i][0] == m:
                pl.when(exists(q + SENDS[i][1]))(lambda i=i: box_copy(i).start())

    send(0)

    def deliver(s, j):
        return pltpu.make_async_remote_copy(
            src_ref=raw.at[s, j], dst_ref=recv.at[first + j],
            send_sem=deliver_sem.at[s, j], recv_sem=recv_sem.at[first + j],
            device_id=(s, q), device_id_type=MESH,
        )

    def deliver_local(s, j):
        return pltpu.make_async_copy(raw.at[s, j], recv.at[first + j], recv_sem.at[first + j])

    def forwards(s):
        return jnp.logical_and(
            jnp.logical_and(core == lax.rem(s, 2), y != s // 2), jnp.logical_and(s >= 1, s < STEPS)
        )

    def forward(s):
        return trans_copy(tall.at[s], s, fsend.at[s], g + 1 - 2 * core)

    def wait_trans(s):
        pltpu.make_async_copy(tall.at[s], tall.at[s], trecv.at[s]).wait()

    def pass_on(s):
        @pl.when(forwards(s))
        def _():
            wait_trans(s)
            forward(s).start()

        each_far_trans(s, lambda c: c.start())

    pass_on(1)

    def tell(i):
        for other in (q + (2 << i), q - (2 << i)):
            @pl.when(exists(other))
            def _():
                pl.semaphore_signal(known.at[i], inc=1, device_id=(g, other), device_id_type=MESH)

    def heard(i):
        count = sum(jnp.where(exists(other), 1, 0) for other in (q + (2 << i), q - (2 << i)))
        pl.semaphore_wait(known.at[i], count)

    tell(0)

    def multiply(s):
        @pl.when(g != s)
        def _():
            pltpu.make_async_copy(mixall.at[s], mixall.at[s], mrecv.at[s]).wait()

        @pl.when(s < g)
        def _():
            amat[...] = jnp.dot(mixall[s][:, :32], amat[...], precision=lax.Precision.HIGHEST, preferred_element_type=F32)


    def step(s, carry):
        for i in range(4):
            @pl.when(s == i + 1)
            def _():
                heard(i)
                if i < 3:
                    tell(i + 1)

        @pl.when(jnp.logical_and(g != s, jnp.logical_not(forwards(s))))
        def _():
            wait_trans(s)

        redo = jnp.logical_and(far, lax.rem(s, 2) == 1)

        for d in range(3):
            t = tall[s, d * B:(d + 1) * B, :].T
            if d == 0:
                t = jnp.where(q > 0, t, jnp.zeros_like(t))
            if d == 2:
                t = jnp.where(q < NQ - 1, t, jnp.zeros_like(t))
            tt[d] = t

        def carry_on(parts, turned, tensor):
            parts = [dot(turned[d], parts[d]).astype(BF16) for d in range(3)]
            return dot(jnp.concatenate(parts, axis=1), tensor).astype(BF16)

        for j in range(SLOTS):
            def body(j=j):
                wait_halo(s, j)
                raw[s + 1, j] = carry_on([halo[s, 0, j], raw[s, j], halo[s, 1, j]], tt, tall[s])

                @pl.when(s < STEPS - 1)
                def _():
                    start_halo(s + 1, j)

                @pl.when(g != s + 1)
                def _():
                    deliver(s + 1, j).start()

                @pl.when(g == s + 1)
                def _():
                    deliver_local(s + 1, j).start()

            each_slot(j, body)

        @pl.when(s == 0)
        def _():
            for i in range(2, STEPS):
                pass_on(i)

            @pl.when(g < STEPS)
            def _():
                for i in range(1, NS):
                    mix_copy(i).start()

        @pl.when(redo)
        def _():
            pltpu.make_async_copy(fart.at[s // 2], fart.at[s // 2], ftrecv.at[s // 2]).wait()
            for d in range(3):
                ft[d] = fart[s // 2, d * B:(d + 1) * B, :].T
            for j in range(SLOTS):
                def again(j=j):
                    halo2_copy(s, j).wait_recv()
                    mine, other = raw[s, j], halo2[s // 2, j]
                    low = jnp.where(x_at == 0, other, mine)
                    high = jnp.where(x_at == 0, mine, other)
                    halo[s + 1, side, j] = carry_on([low, halo[s, side, j], high], ft, fart[s // 2])

                each_slot(j, again)

        pl.when(s >= 3)(lambda: multiply(s - 3))
        return carry

    lax.fori_loop(0, STEPS, step, 0)
    for s in range(STEPS - 3, STEPS):
        multiply(s)

    a = amat[...][:, :32].astype(BF16)
    wide = lax.broadcasted_iota(jnp.int32, (KR, 32), 0) // ROWS
    spread = jnp.where(wide == lax.broadcasted_iota(jnp.int32, (KR, 32), 1), 1.0, 0.0).astype(BF16)
    r0 = lax.rem(lax.broadcasted_iota(jnp.int32, (KR, KR), 0), ROWS)
    r1 = lax.rem(lax.broadcasted_iota(jnp.int32, (KR, KR), 1), ROWS)

    def widen(half):
        full = lax.dot_general(half.astype(BF16), spread, (((1,), (1,)), ((), ())), preferred_element_type=F32)
        return jnp.where(r0 == r1, full, 0.0).astype(BF16)

    turned = widen(lax.dot_general(spread, a, (((1,), (1,)), ((), ())), preferred_element_type=F32))
    loads[3].wait()
    for t in range(B // ROWS):
        rows = renv[:, t * ROWS:(t + 1) * ROWS, :].reshape(KR, B)
        mixed = dot(turned, rows).astype(BF16).reshape(WM, ROWS, B)
        for i, w in enumerate(ORDER):
            at = (i % 2) * B + t * ROWS
            renvp[i // 2, at:at + ROWS, :] = mixed[w]
    big = widen(dot(spread, a))

    def pairs(xx, group):
        acc = None
        for p in group:
            pair = jnp.concatenate([recv[ORDER[2 * p]], recv[ORDER[2 * p + 1]]], axis=1)
            term = dot(dot(pair, xx).astype(BF16), renvp[p])
            acc = term if acc is None else acc + term
        return acc

    def twice(x):
        zero = jnp.zeros_like(x)
        return jnp.concatenate([jnp.concatenate([x, zero], axis=1), jnp.concatenate([zero, x], axis=1)], axis=0)

    def apply(x):
        return pairs(twice(x), range(PAIRS)) * mask

    def largest(v):
        return jnp.max(jnp.max(jnp.abs(v), axis=0, keepdims=True), axis=1, keepdims=True)

    def total(v):
        return jnp.sum(jnp.sum(v, axis=0, keepdims=True), axis=1, keepdims=True)

    def log2(v):
        return jnp.log(jnp.maximum(v, 1e-30)) * 1.4426950408889634

    def norm(v, e):
        up = 2.0 * jnp.floor(0.5 * log2(largest(v)) + 0.5)
        return v * jnp.exp2(-up), e + up

    def add(terms):
        top = terms[0][1]
        for _, e in terms[1:]:
            top = jnp.maximum(top, e)
        value = None
        for m, e in terms:
            part = m * jnp.exp2(e - top)
            value = part if value is None else value + part
        return value, top

    def post(m, value, e):
        outbox[m, :B, :] = value
        outbox[m, B:, :] = jnp.broadcast_to(0.5 * e, (AUX, B)).astype(BF16)
        send(m)

    def take(m, far):
        i = SENDS.index((m, far))
        there = exists(q - far)

        @pl.when(there)
        def _():
            box_copy(i).wait_recv()

        value = jnp.where(there, inbox[i, :B, :].astype(F32), 0.0)
        return value, inbox[i, B:, :].astype(F32)[:1, :1]

    def take_scaled(m, far):
        value, e = take(m, far)
        return value, jnp.where(exists(q - far), 2.0 * e, -1000.0)

    def size(m, e):
        return log2(total(m * m)) + 2.0 * e

    x = outbox[0, :B, :]
    xx = twice(x)
    start_l, rank_l = take(0, 1)
    start_r, rank_r = take(0, -1)
    hop = 0.5 * (start_l + start_r)
    acc = None
    for group in GROUPS:
        for p in group:
            for w in ORDER[2 * p:2 * p + 2]:
                pltpu.make_async_copy(recv.at[w], recv.at[w], recv_sem.at[w]).wait()
        part = pairs(xx, group)
        acc = part if acc is None else acc + part
    m1, l1 = norm(mask * (acc + hop), jnp.zeros((1, 1), F32))
    x1 = m1.astype(BF16)
    post(1, x1, l1)
    mp, lp = norm(apply(x1), l1)
    post(2, mp.astype(BF16), lp)
    sizes = [size(m1, l1)]
    half = 0.5 * mask
    half_l = jnp.where(larger < rank_l, 0.5, 0.0).astype(F32)
    half_r = jnp.where(larger < rank_r, 0.5, 0.0).astype(F32)
    m1_l, l1_l = take_scaled(1, 1)
    m1_r, l1_r = take_scaled(1, -1)
    m2, l2 = norm(*add([(mp, lp), (half * m1_l, l1_l), (half * m1_r, l1_r)]))
    r, lr = norm(apply(m2.astype(BF16)), l2)
    sizes.append(size(m2, l2))
    m1_ll, l1_ll = take_scaled(1, 2)
    m1_rr, l1_rr = take_scaled(1, -2)
    mp_l, lp_l = take_scaled(2, 1)
    mp_r, lp_r = take_scaled(2, -1)
    m2_l, l2_l = add([(mp_l, lp_l), (half_l * m1, l1), (half_l * m1_ll, l1_ll)])
    m2_r, l2_r = add([(mp_r, lp_r), (half_r * m1, l1), (half_r * m1_rr, l1_rr)])
    m2_l, l2_l = jnp.where(low_end, 0.0, m2_l), jnp.where(low_end, -1000.0, l2_l)
    m2_r, l2_r = jnp.where(high_end, 0.0, m2_r), jnp.where(high_end, -1000.0, l2_r)
    m3, l3 = norm(*add([(r, lr), (half * m2_l, l2_l), (half * m2_r, l2_r)]))
    x3 = m3.astype(BF16)
    post(3, x3, l3)
    v, lv = norm(apply(x3), l3)
    sizes.append(size(m3, l3))
    for t in range(B // ROWS):
        rows = recv[:, t * ROWS:(t + 1) * ROWS, :].reshape(KR, B)
        env_out[:, t * ROWS:(t + 1) * ROWS, :] = dot(big, rows).astype(BF16).reshape(WM, ROWS, B)
    m3_l, l3_l = take_scaled(3, 1)
    m3_r, l3_r = take_scaled(3, -1)
    m4, l4 = norm(*add([(v, lv), (half * m3_l, l3_l), (half * m3_r, l3_r)]))
    sizes.append(size(m4, l4))

    lane = lax.broadcasted_iota(jnp.int32, (1, B), 1)
    line = jnp.full((1, B), -1e30, F32)
    for k in range(ITERS):
        line = jnp.where(lane == k, sizes[k] + ((ITERS - 1 - k) * LOG_EPS - LOG_N), line)
    psend[...] = line
    pall[q] = line

    def sum_copy(i):
        return pltpu.make_async_remote_copy(
            src_ref=psend, dst_ref=pall.at[q], send_sem=psem, recv_sem=precv,
            device_id=(g, lax.rem(q + i, NQ)), device_id_type=MESH,
        )

    def start_sum(i, carry):
        sum_copy(i).start()
        return carry

    lax.fori_loop(1, NQ, start_sum, 0)

    def drain(s, carry):
        for j in range(SLOTS):
            def body(j=j):
                each_halo(s, j, lambda c: c.wait_send())
                each_halo2(s, j, lambda c: c.wait_send())

                @pl.when(g != s + 1)
                def _():
                    deliver(s + 1, j).wait_send()

            each_slot(j, body)

        @pl.when(forwards(s))
        def _():
            forward(s).wait_send()

        each_far_trans(s, lambda c: c.wait_send())
        return carry

    lax.fori_loop(0, STEPS, drain, 0)
    each_trans(lambda c: c.wait_send())

    @pl.when(g < STEPS)
    def _():
        for i in range(1, NS):
            mix_copy(i).wait_send()

    for i in range(len(SENDS)):
        pl.when(exists(q + SENDS[i][1]))(lambda i=i: box_copy(i).wait_send())
    others = pall.at[pl.ds(0, NQ - 1)]
    pltpu.make_async_copy(others, others, psem).wait()
    pltpu.make_async_copy(others, others, precv).wait()
    logs = pall[...].reshape(NQ, B)
    top = jnp.max(jnp.max(logs, axis=0, keepdims=True), axis=1, keepdims=True)
    top = jnp.maximum(top, ITERS * LOG_EPS)
    square = total(jnp.exp2(logs - top)) + jnp.exp2(ITERS * LOG_EPS - top)
    state[...] = m4 * (jnp.exp2(l4 - 0.5 * top) * lax.rsqrt(square))


def per_device(env_left, transfer, mpo_mix, right_env, start_state, block_rank):
    dma = pltpu.SemaphoreType.DMA
    vmem = pl.BlockSpec(memory_space=pltpu.VMEM)
    hbm = pl.BlockSpec(memory_space=pltpu.HBM)
    state, env = pl.pallas_call(
        kernel,
        out_shape=(
            jax.ShapeDtypeStruct((B, B), F32),
            jax.ShapeDtypeStruct((WM, B, B), BF16),
        ),
        in_specs=[hbm, hbm, hbm, hbm, hbm, pl.BlockSpec(memory_space=pltpu.SMEM)],
        out_specs=(vmem, vmem),
        scratch_shapes=[
            pltpu.VMEM((NS, SLOTS, B, B), BF16),
            pltpu.VMEM((STEPS, 2, SLOTS, B, B), BF16),
            pltpu.VMEM((3, SLOTS, B, B), BF16),
            pltpu.VMEM((3, 3 * B, B), BF16),
            pltpu.VMEM((3, B, B), BF16),
            pltpu.VMEM((WM, B, B), BF16),
            pltpu.VMEM((WM, B, B), BF16),
            pltpu.VMEM((PAIRS, 2 * B, B), BF16),
            pltpu.VMEM((NS, 3 * B, B), BF16),
            pltpu.VMEM((3, B, B), BF16),
            pltpu.VMEM((NS, 32, B), F32),
            pltpu.VMEM((32, B), F32),
            pltpu.VMEM((WM, 1, WM), F32),
            pltpu.VMEM((32, B), F32),
            pltpu.VMEM((B, B), F32),
            pltpu.VMEM((4, MSG, B), BF16),
            pltpu.VMEM((len(SENDS), MSG, B), BF16),
            pltpu.VMEM((1, B), F32),
            pltpu.VMEM((NQ, 1, B), F32),
            dma((SLOTS,)),
            dma((4,)),
            dma((WM,)),
            dma((NS, SLOTS)),
            dma((STEPS, 2, SLOTS)),
            dma((STEPS, 2, SLOTS)),
            dma((3, SLOTS)),
            dma((3, SLOTS)),
            dma((3,)),
            dma((3, 2)),
            dma((NS,)),
            dma((NS,)),
            dma((NS,)),
            dma((NS,)),
            dma((NS,)),
            dma((len(SENDS),)),
            dma((len(SENDS),)),
            dma,
            dma,
            pltpu.SemaphoreType.REGULAR((4,)),
        ],
        compiler_params=pltpu.CompilerParams(
            collective_id=0, has_side_effects=True, vmem_limit_bytes=40 * 1024 * 1024
        ),
    )(
        *(
            pltpu.with_memory_space_constraint(value, pltpu.HBM)
            for value in (
                env_left.reshape(WM, B, B),
                transfer.reshape(3 * B, B),
                jnp.transpose(mpo_mix, (1, 0, 2)),
                right_env.reshape(WM, B, B),
                start_state.reshape(B, B),
            )
        ),
        block_rank,
    )
    return state.reshape(1, 1, B, B), env.reshape(1, WM, 1, B, B)


def solution(mesh):
    in_specs = (
        P(None, "blk", None, None),
        P("sec", "blk", None, None, None),
        P("sec", None, None),
        P("sec", None, "blk", None, None),
        P("sec", "blk", None, None),
        P("blk"),
    )
    out_specs = (P("sec", "blk", None, None), P("sec", None, "blk", None, None))
    return jax.shard_map(
        per_device, mesh=mesh, in_specs=in_specs, out_specs=out_specs, check_vma=False
    )
```
